32 devices in a mesh: dp: 8 (over z, x), tensor: 4 (over y, core).
Axes of the slice: x: 2, y: 2, z: 4, core: 2. Of those that a mesh axis runs over, the one named last changes fastest.
Arguments:
- encoder_input: bfloat16 [256, 49, 1024], P('dp'), may hold values from -6 to 6
- ln1_gain: bfloat16 [1024], replicated, may hold values from 0.5 to 1.5
- ln1_bias: bfloat16 [1024], replicated, may hold values from -2 to 2
- qkv_weight: bfloat16 [1024, 3, 1024], P(None, None, 'tensor'), may hold values from -0.1875 to 0.1875
- proj_weight: bfloat16 [1024, 1024], P('tensor'), may hold values from -0.5 to 0.5
- ln2_gain: bfloat16 [1024], replicated, may hold values from 0.5 to 1.5
- ln2_bias: bfloat16 [1024], replicated, may hold values from -2 to 2
- fc1_weight: bfloat16 [1024, 4096], P(None, 'tensor'), may hold values from -0.1875 to 0.1875
- fc1_bias: bfloat16 [4096], P('tensor'), may hold values from -2 to 2
- fc2_weight: bfloat16 [4096, 1024], P('tensor'), may hold values from -0.09375 to 0.09375
- embed_weight: bfloat16 [1024, 512], P(None, 'tensor'), may hold values from -0.1875 to 0.1875
- mask_token: bfloat16 [512], P('tensor'), may hold values from -4 to 4
- grid_cotangent: bfloat16 [256, 196, 512], P('dp', None, 'tensor'), may hold values from -6 to 6
- image_order: int32 [256], replicated, may hold values from 0 to 255, as said below
- patch_order: int32 [256, 196], P('dp'), may hold values from 0 to 195, each once within a row
- gsd_index: int32 [256], P('dp'), may hold values from 0 to 15
Outputs:
- grid_features: float32 [256, 196, 512], P('dp', None, 'tensor')
- grad_input: float32 [256, 49, 1024], P('dp')
- grad_ln1_gain: float32 [1024], replicated
- grad_ln1_bias: float32 [1024], replicated
- grad_qkv_weight: float32 [1024, 3, 1024], P('dp', None, 'tensor')
- grad_proj_weight: float32 [1024, 1024], P('tensor', 'dp')
- grad_ln2_gain: float32 [1024], replicated
- grad_ln2_bias: float32 [1024], replicated
- grad_fc1_weight: float32 [1024, 4096], P('dp', 'tensor')
- grad_fc1_bias: float32 [4096], P('tensor')
- grad_fc2_weight: float32 [4096, 1024], P('tensor', 'dp')
- grad_embed_weight: float32 [1024, 512], P('dp', 'tensor')
- grad_mask_token: float32 [512], P('tensor')
The draws below stay inside these ranges and needn't reach their ends.
Inputs may be any that keep to these rules, and one draw needn't show every extreme that they name: `image_order`: A permutation of the 256 images; encoder slot s lies on dp index s // 32, image g on grid device g // 32. Between one encoder device and one grid device there are either no images or exactly 4.
All inputs are finite; a program needn't handle non-finite values.
Results may differ from the reference program's by a relative error of at most 0.022.
Values may be sent and summed in bfloat16 or wider, within the bound.
A program may use at most 192 MiB of HBM per device.

```python
import math
import jax
import jax.numpy as jnp
from jax import lax

D = 1024
HEADS = 16
HEAD_DIM = 64
FF = 4096
DEC = 512
SIDE = 14
NVIS = 49
GSD_LEVELS = 16
IMG_DEV = 32
GRID = 196
IMAGES = 256
N_TENSOR = 4


def swap_front(values, position, target):
    found = jnp.argmax(values == target).astype(jnp.int32)
    first = values[position]
    other = values[found]
    return values.at[found].set(first).at[position].set(other)


def draw_image_order(key, part):
    key = jax.random.fold_in(key, 7)
    offset_key, order_key = jax.random.split(key)
    devices = IMAGES // IMG_DEV
    widest = max(IMG_DEV, devices)
    shuffled = jax.random.permutation(offset_key, widest).astype(jnp.int32)
    shuffled = swap_front(shuffled, 0, 1)
    half_way = devices // 2 if devices > 2 else 0
    shuffled = swap_front(shuffled, 1, half_way)
    if IMG_DEV >= 3 and devices > 3:
        shuffled = swap_front(shuffled, 2, devices - 1)
    offsets = shuffled[:IMG_DEV] % devices
    scores = jax.random.randint(order_key, (devices, IMG_DEV), 0, 1 << 20) * IMG_DEV + jnp.arange(IMG_DEV)[None, :]
    within = jnp.argsort(scores, axis=1)
    sender = jnp.arange(devices)[:, None]
    target = (sender + offsets[None, :]) % devices
    slot_index = jnp.broadcast_to(jnp.arange(IMG_DEV)[None, :], (devices, IMG_DEV))
    image = target * IMG_DEV + within[target, slot_index]
    return image.reshape(-1).astype(jnp.int32)


def with_ends(drawn, key, smallest, top_value):
    longest = drawn.shape.index(max(drawn.shape))
    spots = []
    for shift in (0, 1):
        where = [jax.random.randint(jax.random.fold_in(key, axis), (), 0, length) for axis, length in enumerate(drawn.shape)]
        where[longest] = (where[longest] + shift) % drawn.shape[longest]
        spots.append(tuple(where))
    return drawn.at[spots[0]].set(smallest).at[spots[1]].set(top_value)


def shard_levels(key, shape, cuts, low, high):
    level = 1.0
    for dim, shards_of in cuts:
        steps = jax.random.uniform(jax.random.fold_in(jax.random.fold_in(key, 6), dim), (shards_of,), jnp.float32, low / len(cuts), high / len(cuts))
        level = level * jnp.repeat(jnp.exp(steps), shape[dim] // shards_of).reshape((-1,) + (1,) * (len(shape) - 1 - dim))
    return level


def gaussian(stream_key, extent, spread, limit, pieces=(), kind=jnp.bfloat16):
    gain = shard_levels(stream_key, extent, pieces, -0.22, 0.18) if pieces else 1.0
    drawn = jax.random.normal(stream_key, extent, jnp.float32) * spread * gain
    return jnp.minimum(jnp.maximum(drawn, -limit), limit).astype(kind)


def setup_inputs(seed: int = 0) -> dict:
    key_of = jax.random.split(jax.random.key(seed), 17)
    encoder_input = gaussian(key_of[0], (IMAGES, NVIS, D), 1.0, 6.0, ((0, 8),))
    ln1_gain = jnp.clip(1.0 + 0.1 * jax.random.normal(key_of[1], (D,), jnp.float32), 0.5, 1.5).astype(jnp.bfloat16)
    ln1_bias = gaussian(key_of[2], (D,), 0.3, 2.0)
    qkv_weight = gaussian(key_of[3], (D, 3, D), D ** -0.5, 0.1875, ((2, 4),))
    proj_weight = gaussian(key_of[4], (D, D), (D // 8) ** -0.5, 0.5, ((0, 4),))
    ln2_gain = jnp.clip(1.0 + 0.1 * jax.random.normal(key_of[5], (D,), jnp.float32), 0.5, 1.5).astype(jnp.bfloat16)
    ln2_bias = gaussian(key_of[6], (D,), 0.3, 2.0)
    fc1_weight = gaussian(key_of[7], (D, FF), D ** -0.5, 0.1875, ((1, 4),))
    fc1_bias = gaussian(key_of[8], (FF,), 0.3, 2.0, ((0, 4),))
    fc2_weight = gaussian(key_of[9], (FF, D), FF ** -0.5, 0.09375, ((0, 4),))
    embed_weight = gaussian(key_of[10], (D, DEC), D ** -0.5, 0.1875, ((1, 4),))
    mask_token = gaussian(key_of[11], (DEC,), 1.0, 4.0, ((0, 4),))
    grid_cotangent = gaussian(key_of[12], (IMAGES, GRID, DEC), 1.0, 6.0, ((0, 8), (2, 4)))
    image_order = draw_image_order(jax.random.fold_in(key_of[16], 71), 0)
    patch_order = jax.vmap(lambda own: jax.random.permutation(own, GRID))(jax.random.split(key_of[14], IMAGES)).reshape((IMAGES, GRID)).astype(jnp.int32)
    gsd_index = with_ends(jax.random.randint(key_of[15], (IMAGES,), 0, GSD_LEVELS), jax.random.fold_in(key_of[15], 1), 0, GSD_LEVELS - 1).astype(jnp.int32)
    return dict(encoder_input=encoder_input, ln1_gain=ln1_gain, ln1_bias=ln1_bias, qkv_weight=qkv_weight, proj_weight=proj_weight, ln2_gain=ln2_gain, ln2_bias=ln2_bias, fc1_weight=fc1_weight, fc1_bias=fc1_bias, fc2_weight=fc2_weight, embed_weight=embed_weight, mask_token=mask_token, grid_cotangent=grid_cotangent, image_order=image_order, patch_order=patch_order, gsd_index=gsd_index)


@jax.custom_vjp
def reduced_value(v):
    return lax.optimization_barrier(v.astype(jnp.bfloat16)).astype(jnp.float32)

@jax.custom_vjp
def low_back(v):
    return v

def low_keep(v):
    return (reduced_value(v), None)

def low_pass(kept, grad):
    return (grad,)

def back_keep(v):
    return (v, None)

def back_low(kept, grad):
    return (reduced_value(grad),)
reduced_value.defvjp(low_keep, low_pass)
low_back.defvjp(back_keep, back_low)
EPS = 1e-06
GSD_LOW = 0.3
GSD_HIGH = 10.0
FULL_PRECISION = lax.Precision.HIGHEST

def layer_norm(values, gain_vector, shift_vector):
    row_mean = lax.optimization_barrier(jnp.mean(values, axis=-1, keepdims=True))
    centred = values - row_mean
    variance = lax.optimization_barrier(jnp.mean(centred * centred, axis=-1, keepdims=True))
    return centred * lax.rsqrt(variance + EPS) * gain_vector + shift_vector

def exact_gelu(values):
    return jax.nn.gelu(values, approximate=False)

def grid_positions(level_index, first_column, columns):
    ground_sample = GSD_LOW * jnp.exp(level_index.astype(jnp.float32) * (math.log(GSD_HIGH / GSD_LOW) / (GSD_LEVELS - 1)))
    patch_ids = jnp.arange(GRID)
    patch_row = (patch_ids // SIDE).astype(jnp.float32)
    patch_col = (patch_ids % SIDE).astype(jnp.float32)
    column_ids = first_column + jnp.arange(columns)
    half_width = DEC // 2
    quarter = DEC // 4
    inner_col = column_ids % half_width
    frequency = (inner_col % quarter).astype(jnp.float32)
    angular = jnp.exp(frequency * (-math.log(10000.0) / quarter))
    coordinate = jnp.where((column_ids // half_width)[None, :] == 0, patch_row[:, None], patch_col[:, None])
    phase_angle = ground_sample[:, None, None] * (coordinate * angular[None, :])[None, :, :]
    return jnp.where((inner_col // quarter)[None, None, :] == 1, jnp.cos(phase_angle), jnp.sin(phase_angle))

def pick_rows(lookup_table, row_index):
    return lookup_table[row_index]

def split_rounding(value):
    return low_back(jnp.broadcast_to(value, (N_TENSOR,) + value.shape))

def encode_block(params, block_input):
    gain_one, shift_one, qkv_weight, proj_weight, gain_two, shift_two, fc1_weight, fc1_bias, fc2_weight, embed_weight = params
    block_images = block_input.shape[0]
    total_rows = block_images * NVIS
    head_cols = D // N_TENSOR
    heads_group = HEADS // N_TENSOR
    hidden_cols = FF // N_TENSOR
    embed_cols = DEC // N_TENSOR
    score_scale = HEAD_DIM ** (-0.5)
    inputs_flat = block_input.reshape(total_rows, D)
    normed_one = split_rounding(reduced_value(layer_norm(inputs_flat, gain_one, shift_one)))
    qkv_groups = qkv_weight.reshape(D, 3, N_TENSOR, head_cols).transpose(2, 0, 1, 3)
    projected = jnp.einsum('trd,tdck->trck', normed_one, qkv_groups, precision=FULL_PRECISION)
    projected = reduced_value(low_back(projected)).reshape(N_TENSOR, block_images, NVIS, 3, heads_group, HEAD_DIM)
    queries = projected[:, :, :, 0]
    keys_all = projected[:, :, :, 1]
    values_all = projected[:, :, :, 2]
    scores = low_back(score_scale * jnp.einsum('tbqhe,tbkhe->tbhqk', queries, keys_all, precision=FULL_PRECISION))
    probs_low = reduced_value(jax.nn.softmax(scores, axis=-1))
    attended = jnp.einsum('tbhqk,tbkhe->tbqhe', probs_low, values_all, precision=FULL_PRECISION)
    attended = reduced_value(low_back(attended.reshape(N_TENSOR, total_rows, head_cols)))
    proj_groups = proj_weight.reshape(N_TENSOR, head_cols, D)
    attn_parts = reduced_value(jnp.einsum('trk,tkd->trd', attended, proj_groups, precision=FULL_PRECISION))
    resid_one = inputs_flat + low_back(lax.optimization_barrier(jnp.sum(attn_parts, axis=0)))
    second_normalized = split_rounding(reduced_value(layer_norm(resid_one, gain_two, shift_two)))
    first_dense_groups = fc1_weight.reshape(D, N_TENSOR, hidden_cols).transpose(1, 0, 2)
    raised_value = jnp.einsum('sju,suc->sjc', second_normalized, first_dense_groups, precision=FULL_PRECISION)
    raised_value = low_back(raised_value + fc1_bias.reshape(N_TENSOR, 1, hidden_cols))
    hidden_reduced = reduced_value(exact_gelu(raised_value))
    second_dense_groups = fc2_weight.reshape(N_TENSOR, hidden_cols, D)
    perceptron_pieces = reduced_value(jnp.einsum('bzh,bhi->bzi', hidden_reduced, second_dense_groups, precision=FULL_PRECISION))
    resid_two = resid_one + low_back(lax.optimization_barrier(jnp.sum(perceptron_pieces, axis=0)))
    rounded_out = split_rounding(reduced_value(resid_two))
    embed_groups = embed_weight.reshape(D, N_TENSOR, embed_cols).transpose(1, 0, 2)
    embedded = jnp.einsum('trd,tde->tre', rounded_out, embed_groups, precision=FULL_PRECISION)
    embedded = reduced_value(low_back(embedded))
    return embedded.transpose(1, 0, 2).reshape(block_images, NVIS, DEC)

def reference(encoder_input, ln1_gain, ln1_bias, qkv_weight, proj_weight, ln2_gain, ln2_bias, fc1_weight, fc1_bias, fc2_weight, embed_weight, mask_token, grid_cotangent, image_order, patch_order, gsd_index):
    slot_of_image = jnp.argsort(image_order).astype(jnp.int32)
    patch_rank = jnp.argsort(patch_order, axis=1).astype(jnp.int32)
    is_visible = patch_rank < NVIS
    clipped_rank = jnp.minimum(patch_rank, NVIS - 1).astype(jnp.int32)
    positions = grid_positions(gsd_index, 0, DEC)
    checkpointed = jax.checkpoint(encode_block)

    def forward(inputs_all, gain_one, shift_one, weight_qkv, weight_proj, gain_two, shift_two, weight_up, bias_up, weight_down, weight_embed, token_value):
        params = (gain_one, shift_one, weight_qkv, weight_proj, gain_two, shift_two, weight_up, bias_up, weight_down, weight_embed)
        blocks = inputs_all.reshape(IMAGES // IMG_DEV, IMG_DEV, NVIS, D)

        def run_block(carry_value, block_input):
            return (carry_value, checkpointed(params, block_input))
        unused, embedded = lax.scan(run_block, jnp.zeros((), jnp.float32), blocks)
        embedded = embedded.reshape(IMAGES, NVIS, DEC)
        by_image = embedded[slot_of_image]
        picked = jax.vmap(pick_rows)(by_image, clipped_rank)
        return jnp.where(is_visible[:, :, None], picked, token_value[None, None, :]) + positions
    float_args = (encoder_input.astype(jnp.float32), ln1_gain.astype(jnp.float32), ln1_bias.astype(jnp.float32), qkv_weight.astype(jnp.float32), proj_weight.astype(jnp.float32), ln2_gain.astype(jnp.float32), ln2_bias.astype(jnp.float32), fc1_weight.astype(jnp.float32), fc1_bias.astype(jnp.float32), fc2_weight.astype(jnp.float32), embed_weight.astype(jnp.float32), mask_token.astype(jnp.float32))
    grid_features, pull_back = jax.vjp(forward, *float_args)
    gradients = pull_back(grid_cotangent.astype(jnp.float32))
    return (grid_features, gradients[0], gradients[1], gradients[2], gradients[3], gradients[4], gradients[5], gradients[6], gradients[7], gradients[8], gradients[9], gradients[10], gradients[11])
```

```python
import functools
import math

import jax
import jax.numpy as jnp
from jax import lax
from jax.experimental import pallas as pl
from jax.experimental.pallas import tpu as pltpu
from jax.sharding import PartitionSpec as P

HEAD_DIM = 64
DEC = 512
SIDE = 14
GSD_LEVELS = 16
GRID = 196
NVIS = 49
KPAD = 56
QPAD = 64
GI = 8
EPS = 1e-06
GSD_LOW = 0.3
GSD_HIGH = 10.0
F32 = jnp.float32
BF16 = jnp.bfloat16
SCALE = HEAD_DIM ** (-0.5)
SQRT_HALF = math.sqrt(0.5)
INV_SQRT_2PI = 1.0 / math.sqrt(2.0 * math.pi)
MIB = 1024 * 1024

NT = (((1,), (1,)), ((), ()))
NN = (((1,), (0,)), ((), ()))
TN = (((0,), (0,)), ((), ()))


def dot(a, b, dims=NN):
    return lax.dot_general(a, b, dims, preferred_element_type=F32)


def params(vmem, steps=1):
    if lax.axis_size("dp") != 8:
        vmem = 56
    return pltpu.CompilerParams(
        vmem_limit_bytes=vmem * MIB, dimension_semantics=("arbitrary",) * steps
    )


def cost(flops, nbytes, trans=0):
    return pl.CostEstimate(flops=int(flops), bytes_accessed=int(nbytes), transcendentals=int(trans))


def whole(shape):
    return pl.BlockSpec(shape, lambda *_: (0,) * len(shape))


def normalize(x):
    mean = jnp.mean(x, axis=-1, keepdims=True)
    centred = x - mean
    inv = lax.rsqrt(jnp.mean(centred * centred, axis=-1, keepdims=True) + EPS)
    return centred * inv, inv


def image_rows(x_ref, k0, k1):
    x = x_ref[k0:k1].astype(F32)
    n, _, d = x.shape
    return x[:, :GI].reshape(n * GI, d), x[:, GI:].reshape(n * GI, d)


def head_masks():
    lane = lax.broadcasted_iota(jnp.int32, (1, 4 * HEAD_DIM), 1) // HEAD_DIM
    return [lane == h for h in range(4)]


def stack_heads(v, masks):
    return jnp.concatenate([jnp.where(m, v, 0.0) for m in masks], axis=0).astype(BF16)


def fold_heads(v, masks):
    out = jnp.where(masks[0], v[:QPAD], 0.0)
    for h in range(1, 4):
        out = out + jnp.where(masks[h], v[h * QPAD : (h + 1) * QPAD], 0.0)
    return out


def load_image(ref, j, s, rows):
    return jnp.concatenate(
        [ref[2 * j + l, pl.ds(s, rows, stride=GI), :] for l in range(2)], axis=1
    )


def store_image(ref, j, s, rows, v):
    for l in range(2):
        ref[2 * j + l, pl.ds(s, rows, stride=GI), :] = v[:rows, 128 * l : 128 * (l + 1)]


def softmax_t(keys, stacked):
    st = dot(keys, stacked, NT)
    row = lax.broadcasted_iota(jnp.int32, st.shape, 0)
    st = jnp.where(row < NVIS, st, -1e30)
    e = jnp.exp(st - jnp.max(st, axis=0, keepdims=True))
    return e * (1.0 / jnp.sum(e, axis=0, keepdims=True))


def put_slabs(ref, j, rows, v):
    for l in range(2):
        ref[2 * j + l, 0:rows, :] = v[:, 128 * l : 128 * (l + 1)]


def attn_fwd_kernel(first, rows, meta, *refs):
    if first:
        x_ref, g_ref, b_ref, wq_ref, wp_ref, a_ref, qkv_ref, att_ref, part_ref, sc, osc = refs
        c = meta[1]
        for k0 in range(0, NVIS, 7):
            lo, hi = image_rows(x_ref, k0, k0 + 7)
            own, other = jnp.where(c == 0, lo, hi), jnp.where(c == 0, hi, lo)
            for g, v in enumerate((own, other)):
                a_ref[g, k0 * GI : (k0 + 7) * GI, :] = (
                    normalize(v)[0] * g_ref[...] + b_ref[...]
                ).astype(BF16)
    else:
        a_ref, prev_ref, wq_ref, wp_ref, qkv_ref, att_ref, part_ref, sc, osc = refs
    sc[:, rows:, :] = jnp.zeros((6, sc.shape[1] - rows, 128), F32)
    masks = head_masks()
    for g in (1, 0):
        a = a_ref[g]
        for j in range(3):
            v = dot(a, wq_ref[j]).astype(BF16)
            qkv_ref[j, g] = v
            put_slabs(sc, j, rows, v.astype(F32))

        def image(s, carry):
            q = load_image(sc, 0, s, QPAD) * SCALE
            k = load_image(sc, 1, s, KPAD).astype(BF16)
            v = load_image(sc, 2, s, KPAD).astype(BF16)
            probs = softmax_t(k, stack_heads(q, masks))
            out = dot(probs.T.astype(BF16), v)
            store_image(osc, 0, s, QPAD, fold_heads(out, masks))
            return carry

        lax.fori_loop(0, GI, image, 0, unroll=True)
        att = jnp.concatenate([osc[0, 0:rows, :], osc[1, 0:rows, :]], axis=1).astype(BF16)
        att_ref[g] = att
        part = dot(att, wp_ref[...])
        if not first:
            part = part + prev_ref[g].astype(F32)
        part_ref[g] = part.astype(BF16)


def attn_fwd(meta, first, ins, w_qkv, w_proj):
    d = w_qkv.shape[1]
    hc = w_qkv.shape[2]
    rows = NVIS * GI
    pair = jax.ShapeDtypeStruct((2, rows, d), BF16)
    outs = [
        jax.ShapeDtypeStruct((3, 2, rows, hc), BF16),
        jax.ShapeDtypeStruct((2, rows, hc), BF16),
        pair,
    ]
    if first:
        outs = [pair] + outs
        specs = [
            pl.BlockSpec((NVIS, 2 * GI, d), lambda i, m: (0, m[0], 0)),
            whole((1, d)),
            whole((1, d)),
        ]
    else:
        specs = [whole((2, rows, d)), whole((2, rows, d))]
    specs += [whole((3, d, hc)), whole((hc, d))]
    return pl.pallas_call(
        functools.partial(attn_fwd_kernel, first, rows),
        out_shape=outs,
        grid_spec=pltpu.PrefetchScalarGridSpec(
            num_scalar_prefetch=1,
            grid=(1,),
            in_specs=specs,
            out_specs=[whole(o.shape) for o in outs],
            scratch_shapes=[
                pltpu.VMEM((6, QPAD * GI, 128), F32),
                pltpu.VMEM((2, QPAD * GI, 128), F32),
            ],
        ),
        compiler_params=params(48),
        cost_estimate=cost(2 * 2 * rows * d * hc * 6, 10 * MIB),
        name="attn_fwd",
    )(meta, *ins, w_qkv, w_proj)


def attn_bwd_kernel(first, rows, *refs):
    if first:
        d0_ref, d1_ref, qkv_ref, wq_ref, wp_ref, dqkv_ref, dh_ref, sc, dsc = refs
    else:
        d0_ref, d1_ref, prev_ref, qkv_ref, wq_ref, wp_ref, dqkv_ref, dh_ref, sc, dsc = refs
    sc[:, rows:, :] = jnp.zeros((8, sc.shape[1] - rows, 128), F32)
    masks = head_masks()
    for g in (1, 0):
        d_attn = (d0_ref, d1_ref)[g][...]
        for j in range(3):
            put_slabs(sc, j, rows, qkv_ref[j, g].astype(F32))
        put_slabs(sc, 3, rows, dot(d_attn, wp_ref[...], NT).astype(BF16).astype(F32))

        def image(s, carry):
            q = stack_heads(load_image(sc, 0, s, QPAD) * SCALE, masks)
            k = load_image(sc, 1, s, KPAD).astype(BF16)
            v = load_image(sc, 2, s, KPAD).astype(BF16)
            dh = stack_heads(load_image(sc, 3, s, QPAD), masks)
            probs = softmax_t(k, q)
            d_probs = dot(v, dh, NT)
            d_v = dot(probs.astype(BF16), dh)
            total = jnp.sum(d_probs * probs, axis=0, keepdims=True)
            d_scores = probs * (d_probs - total)
            d_k = dot(d_scores.astype(BF16), q)
            d_q = fold_heads(dot(d_scores.T.astype(BF16), k), masks) * SCALE
            store_image(dsc, 0, s, QPAD, d_q)
            store_image(dsc, 1, s, KPAD, d_k)
            store_image(dsc, 2, s, KPAD, d_v)
            return carry

        lax.fori_loop(0, GI, image, 0, unroll=True)
        total = prev_ref[g].astype(F32) if not first else None
        for j in range(3):
            d_j = jnp.concatenate(
                [dsc[2 * j, 0:rows, :], dsc[2 * j + 1, 0:rows, :]], axis=1
            ).astype(BF16)
            dqkv_ref[j, g] = d_j
            part = dot(d_j, wq_ref[j], NT)
            total = part if total is None else total + part
        dh_ref[g] = total.astype(BF16)


def attn_bwd(d_own, d_other, prev, qkv, w_qkv, w_proj):
    d = w_qkv.shape[1]
    hc = w_qkv.shape[2]
    rows = NVIS * GI
    pair = jax.ShapeDtypeStruct((2, rows, d), BF16)
    first = prev is None
    outs = [jax.ShapeDtypeStruct((3, 2, rows, hc), BF16), pair]
    ins = [d_own, d_other] + ([] if first else [prev]) + [qkv, w_qkv, w_proj]
    return pl.pallas_call(
        functools.partial(attn_bwd_kernel, first, rows),
        out_shape=outs,
        grid=(1,),
        in_specs=[whole(a.shape) for a in ins],
        out_specs=[whole(o.shape) for o in outs],
        scratch_shapes=[
            pltpu.VMEM((8, QPAD * GI, 128), F32),
            pltpu.VMEM((6, QPAD * GI, 128), F32),
        ],
        compiler_params=params(48),
        cost_estimate=cost(2 * 2 * rows * d * hc * 7, 10 * MIB),
        name="attn_bwd",
    )(*ins)


def mlp_kernel(a0, a1, p0, p1, p2, p3, w1, b1, w2, we, mlp, dh2, hid, dup, dmlp, gb):
    i = pl.program_id(0)
    a = jnp.where(i == 0, a0[...], a1[...])
    demb = jnp.concatenate([p0[0], p1[0], p2[0], p3[0]], axis=1)
    dm = dot(demb, we[...], NT).astype(BF16)
    dmlp[0] = dm
    width = w1.shape[1]
    for f in range(0, width, 256):
        cols = slice(f, f + 256)
        up = dot(a, w1[:, cols]) + b1[:, cols]
        cdf = 0.5 * (1.0 + lax.erf(up * SQRT_HALF))
        hid[0, :, cols] = (up * cdf).astype(BF16)
        d_hid = dot(dm, w2[cols, :], NT)
        pdf = jnp.exp(up * up * -0.5) * INV_SQRT_2PI
        d_up = (d_hid * (cdf + up * pdf)).astype(BF16)
        dup[0, :, cols] = d_up
        s = jnp.sum(d_up.astype(F32), axis=0, keepdims=True)
        gb[:, cols] = jnp.where(i == 0, s, gb[:, cols] + s)
    dh2[0] = dot(dup[0], w1[...], NT).astype(BF16)
    mlp[0] = dot(hid[0], w2[...]).astype(BF16)


def mlp_pair(base, a_first, a_second, pieces, w1, b1, w2, we):
    rows, d = a_first.shape
    f = w1.shape[1]
    ec = pieces[0].shape[2]
    pair = jax.ShapeDtypeStruct((2, rows, d), BF16)
    hidden = jax.ShapeDtypeStruct((2, rows, f), BF16)
    step = lambda n: pl.BlockSpec((1, rows, n), lambda i: (i, 0, 0))
    piece = lambda r: pl.BlockSpec((1, rows, ec), lambda i: ((base + i) ^ r, 0, 0))
    return pl.pallas_call(
        mlp_kernel,
        out_shape=[pair, pair, hidden, hidden, pair, jax.ShapeDtypeStruct((1, f), F32)],
        grid=(2,),
        in_specs=[whole((rows, d))] * 2
        + [piece(r) for r in range(4)]
        + [whole(w1.shape), whole(b1.shape), whole(w2.shape), whole(we.shape)],
        out_specs=[step(d), step(d), step(f), step(f), step(d), whole((1, f))],
        compiler_params=params(48),
        cost_estimate=cost(2 * 2 * rows * d * f * 4.5, 18 * MIB, 4 * rows * f),
        name="mlp_pair",
    )(a_first, a_second, *pieces, w1, b1, w2, we)


def own_rows(x_ref, c, k0, k1):
    lo, hi = image_rows(x_ref, k0, k1)
    return jnp.where(c == 0, lo, hi)


def ln2_kernel(meta, x_ref, keep, recv, g_ref, b_ref, x1_ref, a_ref):
    for k0 in range(0, NVIS, 7):
        sl = slice(k0 * GI, (k0 + 7) * GI)
        x1 = own_rows(x_ref, meta[1], k0, k0 + 7) + (
            keep[0, sl, :].astype(F32) + recv[sl, :].astype(F32)
        )
        x1_ref[sl, :] = x1
        a_ref[sl, :] = (normalize(x1)[0] * g_ref[...] + b_ref[...]).astype(BF16)


def ln2(meta, x3, part, recv, gain, shift):
    rows, d = recv.shape
    return pl.pallas_call(
        ln2_kernel,
        out_shape=[jax.ShapeDtypeStruct((rows, d), F32), jax.ShapeDtypeStruct((rows, d), BF16)],
        grid_spec=pltpu.PrefetchScalarGridSpec(
            num_scalar_prefetch=1,
            grid=(1,),
            in_specs=[
                pl.BlockSpec((NVIS, 2 * GI, d), lambda i, m: (0, m[0], 0)),
                pl.BlockSpec((1, rows, d), lambda i, m: (0, 0, 0)),
                whole((rows, d)),
                whole((1, d)),
                whole((1, d)),
            ],
            out_specs=[whole((rows, d)), whole((rows, d))],
        ),
        compiler_params=params(32),
        cost_estimate=cost(20 * rows * d, 6 * MIB),
        name="ln2",
    )(meta, x3, part, recv, gain, shift)


def backward_rows(x, d_out, gain):
    xhat, inv = normalize(x)
    e = d_out * gain
    d_x = inv * (
        e
        - jnp.mean(e, axis=-1, keepdims=True)
        - xhat * jnp.mean(e * xhat, axis=-1, keepdims=True)
    )
    return d_x, jnp.sum(d_out * xhat, axis=0, keepdims=True), jnp.sum(d_out, axis=0, keepdims=True)


def ln2_bwd_kernel(x1, keep, r1, r2, p0, p1, p2, p3, we, g_ref, dx1, dattn, gg, gb):
    rows = x1.shape[0]
    gg[...] = jnp.zeros_like(gg)
    gb[...] = jnp.zeros_like(gb)
    for r0 in range(0, rows, 56):
        sl = slice(r0, r0 + 56)
        demb = jnp.concatenate([p[0, sl, :] for p in (p0, p1, p2, p3)], axis=1)
        d_h = keep[0, sl, :].astype(F32) + r1[sl, :].astype(F32) + r2[sl, :].astype(F32)
        d_x, s_g, s_b = backward_rows(x1[sl, :], d_h, g_ref[...])
        d_x = d_x + dot(demb, we[...], NT)
        dx1[sl, :] = d_x
        dattn[sl, :] = d_x.astype(BF16)
        gg[...] += s_g
        gb[...] += s_b


def ln2_bwd(x1, dh2, r1, r2, pieces, we, gain):
    rows, d = x1.shape
    ec = pieces[0].shape[2]
    piece = lambda r: pl.BlockSpec((1, rows, ec), lambda i: (r, 0, 0))
    vec = jax.ShapeDtypeStruct((1, d), F32)
    return pl.pallas_call(
        ln2_bwd_kernel,
        out_shape=[
            jax.ShapeDtypeStruct((rows, d), F32),
            jax.ShapeDtypeStruct((rows, d), BF16),
            vec,
            vec,
        ],
        grid=(1,),
        in_specs=[
            whole((rows, d)),
            pl.BlockSpec((1, rows, d), lambda i: (0, 0, 0)),
            whole((rows, d)),
            whole((rows, d)),
        ]
        + [piece(r) for r in range(4)]
        + [whole(we.shape), whole((1, d))],
        out_specs=[whole((rows, d)), whole((rows, d)), whole((1, d)), whole((1, d))],
        compiler_params=params(32),
        cost_estimate=cost(2 * rows * d * DEC, 8 * MIB),
        name="ln2_bwd",
    )(x1, dh2, r1, r2, *pieces, we, gain)


def ln1_bwd_kernel(meta, x_ref, dx1, keep, recv, g_ref, out, gg, gb):
    gg[...] = jnp.zeros_like(gg)
    gb[...] = jnp.zeros_like(gb)
    for k0 in range(0, NVIS, 7):
        sl = slice(k0 * GI, (k0 + 7) * GI)
        d_h = keep[0, sl, :].astype(F32) + recv[sl, :].astype(F32)
        d_x, s_g, s_b = backward_rows(own_rows(x_ref, meta[1], k0, k0 + 7), d_h, g_ref[...])
        out[sl, :] = (dx1[sl, :] + d_x).astype(BF16)
        gg[...] += s_g
        gb[...] += s_b


def ln1_bwd(meta, x3, dx1, dh1, recv, gain):
    rows, d = dx1.shape
    vec = jax.ShapeDtypeStruct((1, d), F32)
    return pl.pallas_call(
        ln1_bwd_kernel,
        out_shape=[jax.ShapeDtypeStruct((rows, d), BF16), vec, vec],
        grid_spec=pltpu.PrefetchScalarGridSpec(
            num_scalar_prefetch=1,
            grid=(1,),
            in_specs=[
                pl.BlockSpec((NVIS, 2 * GI, d), lambda i, m: (0, m[0], 0)),
                whole((rows, d)),
                pl.BlockSpec((1, rows, d), lambda i, m: (0, 0, 0)),
                whole((rows, d)),
                whole((1, d)),
            ],
            out_specs=[whole((rows, d)), whole((1, d)), whole((1, d))],
        ),
        compiler_params=params(32),
        cost_estimate=cost(20 * rows * d, 6 * MIB),
        name="ln1_bwd",
    )(meta, x3, dx1, dh1, recv, gain)


def assemble_kernel(meta, g0, g1, g2, g3, out):
    i = pl.program_id(0)
    for r, g in enumerate((g0, g1, g2, g3)):

        @pl.when(i == r)
        def _():
            out[...] = g[...].astype(F32).reshape(out.shape)


def assemble(meta, groups):
    rows, d = groups[0].shape
    return pl.pallas_call(
        assemble_kernel,
        out_shape=jax.ShapeDtypeStruct((NVIS, 4 * GI, d), F32),
        grid_spec=pltpu.PrefetchScalarGridSpec(
            num_scalar_prefetch=1,
            grid=(4,),
            in_specs=[whole((rows, d))] * 4,
            out_specs=pl.BlockSpec((NVIS, GI, d), lambda i, m: (0, i ^ m[2], 0)),
        ),
        compiler_params=params(32),
        cost_estimate=cost(rows * d, 10 * MIB),
        name="assemble",
    )(meta, *groups)


def out_embed_kernel(x1, keep, r1, r2, we, z_ref, emb):
    mlp = keep[0].astype(F32) + r1[...].astype(F32) + r2[...].astype(F32)
    z = (x1[...] + mlp).astype(BF16)
    z_ref[...] = z
    e = dot(z, we[...]).astype(BF16)
    ec = emb.shape[2]
    for q in range(4):
        emb[q] = e[:, q * ec : (q + 1) * ec]


def out_embed(x1, mlp, r1, r2, we):
    rows, d = x1.shape
    ec = we.shape[1] // 4
    return pl.pallas_call(
        out_embed_kernel,
        out_shape=[
            jax.ShapeDtypeStruct((rows, d), BF16),
            jax.ShapeDtypeStruct((4, rows, ec), BF16),
        ],
        grid=(1,),
        in_specs=[
            whole((rows, d)),
            pl.BlockSpec((1, rows, d), lambda i: (0, 0, 0)),
            whole((rows, d)),
            whole((rows, d)),
            whole(we.shape),
        ],
        out_specs=[whole((rows, d)), whole((4, rows, ec))],
        compiler_params=params(32),
        cost_estimate=cost(2 * rows * d * DEC, 6 * MIB),
        name="out_embed",
    )(x1, mlp, r1, r2, we)


def collect_kernel(recv_index, cot, po, rows_out, token, csc):
    csc[...] = cot[...].astype(F32).reshape(csc.shape)
    total = jnp.sum(csc[...], axis=0, keepdims=True)
    if rows_out.shape[0] > cot.shape[1]:
        rows_out[...] = jnp.zeros_like(rows_out)
    images = cot.shape[1]
    lane = lax.broadcasted_iota(jnp.int32, (KPAD, GRID), 1)

    def image(g, seen):
        cells = csc[pl.ds(g, GRID, stride=images), :].astype(BF16)
        pick = jnp.where(po[g] == lane, 1.0, 0.0).astype(BF16)
        v = dot(pick, cells)
        rows_out[recv_index[g]] = v.astype(BF16)
        return seen + jnp.sum(v, axis=0, keepdims=True)

    seen = lax.fori_loop(0, images, image, jnp.zeros((1, 128), F32), unroll=4)
    token[...] = total - seen


def collect(recv_index, cot, po_cols, slots):
    return pl.pallas_call(
        collect_kernel,
        out_shape=[
            jax.ShapeDtypeStruct((slots, KPAD, 128), BF16),
            jax.ShapeDtypeStruct((1, 128), F32),
        ],
        grid_spec=pltpu.PrefetchScalarGridSpec(
            num_scalar_prefetch=1,
            grid=(1,),
            in_specs=[whole(cot.shape), whole(po_cols.shape)],
            out_specs=[whole((slots, KPAD, 128)), whole((1, 128))],
            scratch_shapes=[pltpu.VMEM((GRID * cot.shape[1], 128), F32)],
        ),
        compiler_params=params(32),
        cost_estimate=cost(2 * 32 * KPAD * GRID * 128, 4 * MIB),
        name="collect",
    )(recv_index, cot, po_cols)


def to_rows_kernel(meta, index, slots, out, sc):
    rows = out.shape[1]
    for s in range(4 * GI):
        v = slots[index[s]].astype(F32)
        sc[(s // GI) ^ meta[2], pl.ds(s % GI, KPAD, stride=GI), :] = v
    out[...] = sc[:, 0:rows, :].astype(BF16)


def to_rows(meta, index, slots):
    rows = NVIS * GI
    return pl.pallas_call(
        to_rows_kernel,
        out_shape=jax.ShapeDtypeStruct((4, rows, 128), BF16),
        grid_spec=pltpu.PrefetchScalarGridSpec(
            num_scalar_prefetch=2,
            grid=(1,),
            in_specs=[whole(slots.shape)],
            out_specs=whole((4, rows, 128)),
            scratch_shapes=[pltpu.VMEM((4, KPAD * GI, 128), F32)],
        ),
        compiler_params=params(16),
        cost_estimate=cost(4 * rows * 128, MIB),
        name="to_rows",
    )(meta, index, slots)


def to_slots_kernel(meta, index, e0, e1, e2, e3, out, sc):
    rows = e0.shape[-2]
    for r, e in enumerate((e0, e1, e2, e3)):
        sc[r, 0:rows, :] = e[...].reshape(rows, 128).astype(F32)
    sc[:, rows:, :] = jnp.zeros((4, KPAD * GI - rows, 128), F32)
    if out.shape[0] > 4 * GI:
        out[...] = jnp.zeros_like(out)
    for s in range(4 * GI):
        v = sc[(s // GI) ^ meta[2], pl.ds(s % GI, KPAD, stride=GI), :]
        out[index[s]] = v.astype(BF16)


def to_slots(meta, index, emb, received, slots):
    rows = NVIS * GI
    return pl.pallas_call(
        to_slots_kernel,
        out_shape=jax.ShapeDtypeStruct((slots, KPAD, 128), BF16),
        grid_spec=pltpu.PrefetchScalarGridSpec(
            num_scalar_prefetch=2,
            grid=(1,),
            in_specs=[pl.BlockSpec((1, rows, 128), lambda *_: (0, 0, 0))] + [whole((rows, 128))] * 3,
            out_specs=whole((slots, KPAD, 128)),
            scratch_shapes=[pltpu.VMEM((4, KPAD * GI, 128), F32)],
        ),
        compiler_params=params(16),
        cost_estimate=cost(4 * rows * 128, MIB),
        name="to_slots",
    )(meta, index, emb, *received)


def grid_kernel(meta, index, slots, po, token, table, out, sc):
    images = out.shape[1]
    cell = lax.broadcasted_iota(jnp.int32, (GRID, KPAD), 0)
    ones = jnp.ones((KPAD, 128), BF16)

    def image(g, carry):
        pick = jnp.where(po[g] == cell, 1.0, 0.0).astype(BF16)
        both = dot(pick, jnp.concatenate([slots[index[g]], ones], axis=1))
        v = jnp.where(both[:, 128:] > 0.5, both[:, :128], token[...])
        sc[pl.ds(g, GRID, stride=images), :] = v
        return carry

    lax.fori_loop(0, images, image, 0, unroll=4)

    def line(i, carry):
        for j in range(SIDE):
            u = jnp.where(meta[2] < 2, i, j)
            p = i * SIDE + j
            start = pl.multiple_of(p * images, images)
            out[p] = sc[pl.ds(start, images), :] + table[u]
        return carry

    lax.fori_loop(0, SIDE, line, 0)


def grid_out(meta, index, slots, po_rows, token, table):
    images = table.shape[1]
    return pl.pallas_call(
        grid_kernel,
        out_shape=jax.ShapeDtypeStruct((GRID, images, 128), F32),
        grid_spec=pltpu.PrefetchScalarGridSpec(
            num_scalar_prefetch=2,
            grid=(1,),
            in_specs=[whole(slots.shape), whole(po_rows.shape), whole((1, 128)), whole(table.shape)],
            out_specs=whole((GRID, images, 128)),
            scratch_shapes=[pltpu.VMEM((GRID * images, 128), F32)],
        ),
        compiler_params=params(32),
        cost_estimate=cost(2 * 32 * KPAD * GRID * 256, 5 * MIB),
        name="grid_out",
    )(meta, index, slots, po_rows, token, table)


def position_table(level_index, part):
    sample = GSD_LOW * jnp.exp(
        level_index.astype(F32) * (math.log(GSD_HIGH / GSD_LOW) / (GSD_LEVELS - 1))
    )
    quarter = DEC // 4
    angular = jnp.exp(jnp.arange(quarter).astype(F32) * (-math.log(10000.0) / quarter))
    coordinate = jnp.arange(SIDE).astype(F32)
    phase = sample[None, :, None] * (coordinate[:, None] * angular[None, :])[:, None, :]
    return jnp.where(part % 2 == 1, jnp.cos(phase), jnp.sin(phase))


def after(v, *others):
    return lax.optimization_barrier((v,) + others)[0]


def grad_kernel(split_rows, n, *refs):
    a_refs, b_refs, out = refs[:n], refs[n : 2 * n], refs[2 * n]
    total = None
    for a, b in zip(a_refs, b_refs):
        for g in range(a.shape[0]):
            t = dot(a[g], b[g], TN)
            total = t if total is None else total + t
    half = (total.shape[0] if split_rows else total.shape[1]) // 2
    for x in range(2):
        sl = slice(x * half, (x + 1) * half)
        out[x, 0] = (total[sl, :] if split_rows else total[:, sl]).astype(BF16)


def grad_weight(a_list, b_list, split_rows):
    rows = a_list[0].shape[1]
    m, n = a_list[0].shape[2], b_list[0].shape[2]
    if split_rows:
        a_spec = lambda g: pl.BlockSpec((g, rows, m // 4), lambda i: (0, 0, i))
        b_spec = lambda g: pl.BlockSpec((g, rows, n), lambda i: (0, 0, 0))
        shape = (2, 4, m // 8, n)
    else:
        a_spec = lambda g: pl.BlockSpec((g, rows, m), lambda i: (0, 0, 0))
        b_spec = lambda g: pl.BlockSpec((g, rows, n // 4), lambda i: (0, 0, i))
        shape = (2, 4, m, n // 8)
    return pl.pallas_call(
        functools.partial(grad_kernel, split_rows, len(a_list)),
        out_shape=jax.ShapeDtypeStruct(shape, BF16),
        grid=(4,),
        in_specs=[a_spec(a.shape[0]) for a in a_list] + [b_spec(b.shape[0]) for b in b_list],
        out_specs=pl.BlockSpec((2, 1) + shape[2:], lambda i: (0, i, 0, 0)),
        compiler_params=params(48),
        cost_estimate=cost(2 * rows * m * n * sum(a.shape[0] for a in a_list), 8 * MIB),
        name="grad_weight",
    )(*a_list, *b_list)


def grad_qkv_kernel(a_ref, b_ref, out):
    cols = b_ref.shape[3]
    half = out.shape[2]
    for j in range(3):
        total = dot(a_ref[0], b_ref[j, 0], TN) + dot(a_ref[1], b_ref[j, 1], TN)
        for x in range(2):
            out[x, 0, :, j * cols : (j + 1) * cols] = total[x * half : (x + 1) * half].astype(BF16)


def grad_qkv_weight(a, b):
    _, rows, m = a.shape
    cols = b.shape[3]
    shape = (2, 4, m // 8, 3 * cols)
    return pl.pallas_call(
        grad_qkv_kernel,
        out_shape=jax.ShapeDtypeStruct(shape, BF16),
        grid=(4,),
        in_specs=[pl.BlockSpec((2, rows, m // 4), lambda i: (0, 0, i)), whole(b.shape)],
        out_specs=pl.BlockSpec((2, 1) + shape[2:], lambda i: (0, i, 0, 0)),
        compiler_params=params(32),
        cost_estimate=cost(2 * 2 * rows * m * 3 * cols, 6 * MIB),
        name="grad_qkv",
    )(a, b)


def local(
    encoder_input,
    ln1_gain,
    ln1_bias,
    qkv_weight,
    proj_weight,
    ln2_gain,
    ln2_bias,
    fc1_weight,
    fc1_bias,
    fc2_weight,
    embed_weight,
    mask_token,
    grid_cotangent,
    image_order,
    patch_order,
    gsd_index,
):
    ndp = lax.axis_size("dp")
    d = lax.axis_index("dp")
    t = lax.axis_index("tensor")
    images, _, width = encoder_input.shape
    rows = NVIS * GI
    xbit, zpos = d % 2, d // 2
    meta = jnp.stack([t // 2, t % 2, t]).astype(jnp.int32)

    def over_core(v):
        return lax.ppermute(v, "tensor", [(i, i ^ 1) for i in range(4)])

    def over_y(v):
        return lax.ppermute(v, "tensor", [(i, i ^ 2) for i in range(4)])

    def over_x(v):
        return lax.ppermute(v, "dp", [(i, i ^ 1) for i in range(ndp)])

    pick = functools.partial(lax.dynamic_index_in_dim, axis=0, keepdims=False)

    g1 = ln1_gain.astype(F32)[None, :]
    s1 = ln1_bias.astype(F32)[None, :]
    g2 = ln2_gain.astype(F32)[None, :]
    s2 = ln2_bias.astype(F32)[None, :]
    bias_up = fc1_bias.astype(F32)[None, :]
    x3 = encoder_input.transpose(1, 0, 2)
    cot = grid_cotangent.transpose(1, 0, 2)
    w_qkv = qkv_weight.transpose(1, 0, 2)

    def y_half(w, axis):
        half = w.shape[axis] // 2
        return over_y(lax.dynamic_slice_in_dim(w, xbit * half, half, axis))

    def both_halves(mine, axis):
        other = over_x(mine)
        lo = jnp.where(xbit == 0, mine, other)
        hi = jnp.where(xbit == 0, other, mine)
        return jnp.concatenate([lo, hi], axis=axis)

    half_qkv = y_half(w_qkv, 1)
    half_proj = y_half(proj_weight, 0)
    w_qkv_far = both_halves(half_qkv, 1)
    w_proj_far = both_halves(half_proj, 0)
    we_core = over_core(embed_weight)
    we_y = over_y(embed_weight)
    we = jnp.concatenate([embed_weight, we_core, we_y, over_core(we_y)], axis=1)

    capacity = max(1, images // ndp)
    slots = ndp * capacity
    own_images = lax.dynamic_slice_in_dim(image_order, d * images, images)
    dest = own_images // images
    before = jnp.arange(images)[None, :] < jnp.arange(images)[:, None]
    rank = jnp.sum((dest[:, None] == dest[None, :]) & before, axis=1)
    send_index = (dest * capacity + rank).astype(jnp.int32)
    every = jnp.arange(image_order.shape[0])
    wanted = d * images + jnp.arange(images)
    slot = jnp.sum(jnp.where(image_order[None, :] == wanted[:, None], every[None, :], 0), axis=1)
    source = slot // images
    to_me = image_order // images == d
    earlier = (
        to_me[None, :]
        & (every[None, :] // images == source[:, None])
        & (every[None, :] < slot[:, None])
    )
    recv_index = (source * capacity + jnp.sum(earlier, axis=1)).astype(jnp.int32)

    visible = jnp.pad(
        patch_order[:, :NVIS], ((0, 0), (0, KPAD - NVIS)), constant_values=-1
    )

    def over_dp(v):
        return lax.all_to_all(v, "dp", split_axis=0, concat_axis=0, tiled=True)

    back, token_grad = collect(recv_index, cot, visible[:, :, None], slots)
    p0 = to_rows(meta, send_index, over_dp(back))
    p1, p2 = over_core(p0), over_y(p0)
    p3 = over_core(p2)
    pieces = (p0, p1, p2, p3)

    a1, qkv_a, att_a, part_a = attn_fwd(
        meta, True, [x3, after(g1, half_qkv, half_proj), s1], w_qkv, proj_weight
    )
    qkv_b, att_b, part = attn_fwd(meta, False, [a1, part_a], w_qkv_far, w_proj_far)
    x1, a2 = ln2(meta, x3, part, over_core(part[1]), g2, s2)
    a2_y = over_y(a2)
    a2_core = over_core(a2)

    mlp_n, dh_n, hid_n, dup_n, dm_n, gb_n = mlp_pair(
        0, a2, a2_core, pieces, fc1_weight, bias_up, fc2_weight, we
    )
    a2_y = after(a2_y, dh_n)
    a2_far = over_core(a2_y)
    mlp_f, dh_f, hid_f, dup_f, dm_f, gb_f = mlp_pair(
        2, a2_y, a2_far, pieces, fc1_weight, bias_up, fc2_weight, we
    )

    def scatter_rows(near, far):
        from_core = over_core(near[1])
        for_y = (far[0].astype(F32) + over_core(far[1]).astype(F32)).astype(BF16)
        return from_core, over_y(for_y)

    r1, r2 = scatter_rows(dh_n, dh_f)
    dx1, d_attn, gg2, gs2 = ln2_bwd(x1, dh_n, r1, r2, pieces, we, g2)
    d_attn_core = over_core(d_attn)
    dqkv_b, dh1_b = attn_bwd(d_attn, d_attn_core, None, qkv_b, w_qkv_far, w_proj_far)
    dqkv_a, dh1 = attn_bwd(d_attn, d_attn_core, dh1_b, qkv_a, w_qkv, proj_weight)
    g_own, gg1, gs1 = ln1_bwd(meta, x3, dx1, dh1, over_core(dh1[1]), g1)
    g_core, g_y = over_core(g_own), over_y(g_own)
    grad_input = assemble(meta, (g_own, g_core, g_y, over_core(g_y)))

    m1, m2 = scatter_rows(mlp_n, mlp_f)
    z, emb = out_embed(x1, mlp_n, m1, m2, we)
    e2 = over_y(jnp.stack([emb[2], emb[3]]))
    received = (over_core(emb[1]), e2[0], over_core(e2[1]))
    arrived = over_dp(to_slots(meta, send_index, emb, received, slots))
    grid_features = grid_out(
        meta,
        recv_index,
        arrived,
        visible[:, None, :],
        mask_token.astype(F32)[None, :],
        position_table(gsd_index, t),
    )

    def sum_dp(v, rest):
        if ndp != 8:
            flat = v.swapaxes(0, 1).reshape((8,) + v.shape[2:])
            if rest == 0:
                whole_v = flat.reshape((8 * v.shape[2],) + v.shape[3:])
                return lax.psum_scatter(whole_v, "dp", scatter_dimension=0, tiled=True).astype(F32)
            whole_v = jnp.concatenate([flat[i] for i in range(8)], axis=1)
            return lax.psum_scatter(whole_v, "dp", scatter_dimension=1, tiled=True).astype(F32)
        got = over_x(pick(v, 1 - xbit))
        u = (pick(v, xbit).astype(F32) + got.astype(F32)).astype(BF16)
        total = pick(u, zpos).astype(F32)
        for s in range(1, 4):
            total = total + lax.ppermute(
                pick(u, zpos ^ s), "dp", [(i, i ^ (2 * s)) for i in range(8)]
            ).astype(F32)
        return total

    grad_fc2 = sum_dp(grad_weight([hid_n, hid_f], [dm_n, dm_f], False), 1)
    a2_parts = [a2[None], a2_core[None], a2_y[None], a2_far[None]]
    dup_parts = [dup_n[0:1], dup_n[1:2], dup_f[0:1], dup_f[1:2]]
    grad_fc1 = sum_dp(grad_weight(a2_parts, dup_parts, True), 0)

    d_pair = [d_attn[None], d_attn_core[None]]

    def over_pair(near, far):
        return near + over_y(far.astype(BF16)).astype(F32)

    att_pairs = lambda v: [v[0:1], v[1:2]]
    grad_proj = over_pair(
        sum_dp(grad_weight(att_pairs(att_a), d_pair, False), 1),
        sum_dp(grad_weight(att_pairs(att_b), d_pair, False), 1),
    )
    grad_qkv = over_pair(
        sum_dp(grad_qkv_weight(a1, dqkv_a), 0), sum_dp(grad_qkv_weight(a1, dqkv_b), 0)
    )
    hc = qkv_weight.shape[2]
    grad_qkv = jnp.stack([grad_qkv[:, j * hc : (j + 1) * hc] for j in range(3)], axis=1)

    demb_own = jnp.concatenate([p[r : r + 1] for r, p in enumerate(pieces)], axis=2)
    ge = grad_weight([z[None]], [demb_own], True)
    ec = embed_weight.shape[1]
    ge_core = over_core(
        jnp.concatenate([ge[..., ec : 2 * ec], ge[..., 3 * ec :]], axis=-1)
    )
    ge_two = jnp.concatenate([ge[..., :ec], ge[..., 2 * ec : 3 * ec]], axis=-1)
    ge_two = sum_dp((ge_two.astype(F32) + ge_core.astype(F32)).astype(BF16), 0)
    grad_embed = over_pair(ge_two[:, :ec], ge_two[:, ec:])

    small = jnp.concatenate(
        [gg1, gs1, gg2, gs2, gb_n + gb_f, jnp.pad(token_grad, ((0, 0), (0, width - 128)))], axis=0
    )
    step = 1
    while step < ndp:
        small = small + lax.ppermute(small, "dp", [(i, i ^ step) for i in range(ndp)])
        step *= 2
    sums = small[:4] + over_core(small[:4])
    sums = sums + over_y(sums)
    gb, token_sum = small[4:5], small[5:6, :128]
    return (
        grid_features.transpose(1, 0, 2),
        grad_input.transpose(1, 0, 2),
        sums[0],
        sums[1],
        grad_qkv,
        grad_proj,
        sums[2],
        sums[3],
        grad_fc1,
        gb[0],
        grad_fc2,
        grad_embed,
        token_sum[0],
    )


def solution(mesh):
    return jax.shard_map(
        local,
        mesh=mesh,
        in_specs=(
            P("dp", None, None),
            P(),
            P(),
            P(None, None, "tensor"),
            P("tensor", None),
            P(),
            P(),
            P(None, "tensor"),
            P("tensor"),
            P("tensor", None),
            P(None, "tensor"),
            P("tensor"),
            P("dp", None, "tensor"),
            P(),
            P("dp", None),
            P("dp"),
        ),
        out_specs=(
            P("dp", None, "tensor"),
            P("dp", None, None),
            P(),
            P(),
            P("dp", None, "tensor"),
            P("tensor", "dp"),
            P(),
            P(),
            P("dp", "tensor"),
            P("tensor"),
            P("tensor", "dp"),
            P("dp", "tensor"),
            P("tensor"),
        ),
        check_vma=False,
    )
```

```python
import functools
import itertools
import math
import types

import jax
import jax.numpy as jnp
from jax import lax
from jax.experimental import pallas as pl
from jax.experimental.pallas import tpu as pltpu
from jax.sharding import PartitionSpec as P

HEAD_DIM = 64
DEC = 512
SIDE = 14
GSD_LEVELS = 16
GRID = 196
NVIS = 49
KPAD = 56
QPAD = 64
GI = 8
EPS = 1e-06
GSD_LOW = 0.3
GSD_HIGH = 10.0
F32 = jnp.float32
BF16 = jnp.bfloat16
SCALE = HEAD_DIM ** (-0.5)
SQRT_HALF = math.sqrt(0.5)
INV_SQRT_2PI = 1.0 / math.sqrt(2.0 * math.pi)
MIB = 1024 * 1024

NT = (((1,), (1,)), ((), ()))
NN = (((1,), (0,)), ((), ()))
TN = (((0,), (0,)), ((), ()))


def dot(a, b, dims=NN):
    return lax.dot_general(a, b, dims, preferred_element_type=F32)


def params(vmem, steps=1):
    if lax.axis_size("dp") != 8:
        vmem = 56
    return pltpu.CompilerParams(
        vmem_limit_bytes=vmem * MIB, dimension_semantics=("arbitrary",) * steps
    )


def cost(flops, nbytes, trans=0):
    return pl.CostEstimate(flops=int(flops), bytes_accessed=int(nbytes), transcendentals=int(trans))


def whole(shape):
    return pl.BlockSpec(shape, lambda *_: (0,) * len(shape))


def normalize(x):
    mean = jnp.mean(x, axis=-1, keepdims=True)
    centred = x - mean
    inv = lax.rsqrt(jnp.mean(centred * centred, axis=-1, keepdims=True) + EPS)
    return centred * inv, inv


def image_rows(x_ref, k0, k1):
    x = x_ref[k0:k1].astype(F32)
    n, _, d = x.shape
    return x[:, :GI].reshape(n * GI, d), x[:, GI:].reshape(n * GI, d)


def head_masks():
    lane = lax.broadcasted_iota(jnp.int32, (1, 4 * HEAD_DIM), 1) // HEAD_DIM
    return [lane == h for h in range(4)]


def stack_heads(v, masks):
    return jnp.concatenate([jnp.where(m, v, 0.0) for m in masks], axis=0).astype(BF16)


def fold_heads(v, masks):
    out = jnp.where(masks[0], v[:QPAD], 0.0)
    for h in range(1, 4):
        out = out + jnp.where(masks[h], v[h * QPAD : (h + 1) * QPAD], 0.0)
    return out


def load_image(ref, j, s, rows):
    return jnp.concatenate(
        [ref[2 * j + l, pl.ds(s, rows, stride=GI), :] for l in range(2)], axis=1
    )


def store_image(ref, j, s, rows, v):
    for l in range(2):
        ref[2 * j + l, pl.ds(s, rows, stride=GI), :] = v[:rows, 128 * l : 128 * (l + 1)]


def softmax_t(keys, stacked):
    st = dot(keys, stacked, NT)
    row = lax.broadcasted_iota(jnp.int32, st.shape, 0)
    st = jnp.where(row < NVIS, st, -1e30)
    e = jnp.exp(st - jnp.max(st, axis=0, keepdims=True))
    return e * (1.0 / jnp.sum(e, axis=0, keepdims=True))


def put_slabs(ref, j, rows, v):
    for l in range(2):
        ref[2 * j + l, 0:rows, :] = v[:, 128 * l : 128 * (l + 1)]


def attn_fwd_kernel(first, rows, meta, *refs):
    if first:
        x_ref, g_ref, b_ref, wq_ref, wp_ref, a_ref, qkv_ref, att_ref, own_ref, other_ref, sc, osc = refs
        c = meta[1]
        for k0 in range(0, NVIS, 7):
            lo, hi = image_rows(x_ref, k0, k0 + 7)
            own, other = jnp.where(c == 0, lo, hi), jnp.where(c == 0, hi, lo)
            for g, v in enumerate((own, other)):
                a_ref[g, k0 * GI : (k0 + 7) * GI, :] = (
                    normalize(v)[0] * g_ref[...] + b_ref[...]
                ).astype(BF16)
    else:
        a_ref, prev0, prev1, wq_ref, wp_ref, qkv_ref, att_ref, own_ref, other_ref, sc, osc = refs
    sc[:, rows:, :] = jnp.zeros((6, sc.shape[1] - rows, 128), F32)
    masks = head_masks()
    for g in (1, 0):
        a = a_ref[g]
        for j in range(3):
            v = dot(a, wq_ref[j]).astype(BF16)
            qkv_ref[j, g] = v
            put_slabs(sc, j, rows, v.astype(F32))

        def image(s, carry):
            q = load_image(sc, 0, s, QPAD) * SCALE
            k = load_image(sc, 1, s, KPAD).astype(BF16)
            v = load_image(sc, 2, s, KPAD).astype(BF16)
            probs = softmax_t(k, stack_heads(q, masks))
            out = dot(probs.T.astype(BF16), v)
            store_image(osc, 0, s, QPAD, fold_heads(out, masks))
            return carry

        lax.fori_loop(0, GI, image, 0, unroll=True)
        att = jnp.concatenate([osc[0, 0:rows, :], osc[1, 0:rows, :]], axis=1).astype(BF16)
        att_ref[g] = att
        part = dot(att, wp_ref[...])
        if not first:
            part = part + (prev0, prev1)[g][...].astype(F32)
        (own_ref, other_ref)[g][...] = part.astype(BF16)


def attn_fwd(meta, first, ins, w_qkv, w_proj):
    d = w_qkv.shape[1]
    hc = w_qkv.shape[2]
    rows = NVIS * GI
    pair = jax.ShapeDtypeStruct((2, rows, d), BF16)
    outs = [
        jax.ShapeDtypeStruct((3, 2, rows, hc), BF16),
        jax.ShapeDtypeStruct((2, rows, hc), BF16),
        jax.ShapeDtypeStruct((rows, d), BF16),
        jax.ShapeDtypeStruct((rows, d), BF16),
    ]
    if first:
        outs = [pair] + outs
        specs = [
            pl.BlockSpec((NVIS, 2 * GI, d), lambda i, m: (0, m[0], 0)),
            whole((1, d)),
            whole((1, d)),
        ]
    else:
        specs = [whole((2, rows, d)), whole((rows, d)), whole((rows, d))]
    specs += [whole((3, d, hc)), whole((hc, d))]
    return pl.pallas_call(
        functools.partial(attn_fwd_kernel, first, rows),
        out_shape=outs,
        grid_spec=pltpu.PrefetchScalarGridSpec(
            num_scalar_prefetch=1,
            grid=(1,),
            in_specs=specs,
            out_specs=[whole(o.shape) for o in outs],
            scratch_shapes=[
                pltpu.VMEM((6, QPAD * GI, 128), F32),
                pltpu.VMEM((2, QPAD * GI, 128), F32),
            ],
        ),
        compiler_params=params(48),
        cost_estimate=cost(2 * 2 * rows * d * hc * 6, 10 * MIB),
        name="attn_fwd",
    )(meta, *ins, w_qkv, w_proj)


def attn_bwd_image(sc, dsc, masks, s, carry):
    q = stack_heads(load_image(sc, 0, s, QPAD) * SCALE, masks)
    k = load_image(sc, 1, s, KPAD).astype(BF16)
    v = load_image(sc, 2, s, KPAD).astype(BF16)
    dh = stack_heads(load_image(sc, 3, s, QPAD), masks)
    probs = softmax_t(k, q)
    d_probs = dot(v, dh, NT)
    d_v = dot(probs.astype(BF16), dh)
    total = jnp.sum(d_probs * probs, axis=0, keepdims=True)
    d_scores = probs * (d_probs - total)
    d_k = dot(d_scores.astype(BF16), q)
    d_q = fold_heads(dot(d_scores.T.astype(BF16), k), masks) * SCALE
    store_image(dsc, 0, s, QPAD, d_q)
    store_image(dsc, 1, s, KPAD, d_k)
    store_image(dsc, 2, s, KPAD, d_v)
    return carry


def attn_bwd_kernel(first, rows, *refs):
    if first:
        d0_ref, d1_ref, qkv_ref, wq_ref, wp_ref, dqkv_ref, own_ref, other_ref, sc, dsc = refs
    else:
        (
            d0_ref, d1_ref, prev0, prev1, qkv_ref, wq_ref, wp_ref,
            dqkv_ref, own_ref, other_ref, sc, dsc,
        ) = refs
    sc[:, rows:, :] = jnp.zeros((8, sc.shape[1] - rows, 128), F32)
    masks = head_masks()
    for g in (1, 0):
        d_attn = (d0_ref, d1_ref)[g][...]
        for j in range(3):
            put_slabs(sc, j, rows, qkv_ref[j, g].astype(F32))
        put_slabs(sc, 3, rows, dot(d_attn, wp_ref[...], NT).astype(BF16).astype(F32))

        def image(s, carry):
            return attn_bwd_image(sc, dsc, masks, s, carry)

        lax.fori_loop(0, GI, image, 0, unroll=True)
        total = (prev0, prev1)[g][...].astype(F32) if not first else None
        for j in range(3):
            d_j = jnp.concatenate(
                [dsc[2 * j, 0:rows, :], dsc[2 * j + 1, 0:rows, :]], axis=1
            ).astype(BF16)
            dqkv_ref[j, g] = d_j
            part = dot(d_j, wq_ref[j], NT)
            total = part if total is None else total + part
        (own_ref, other_ref)[g][...] = total.astype(BF16)


def attn_bwd(d_own, d_other, prev, qkv, w_qkv, w_proj):
    d = w_qkv.shape[1]
    hc = w_qkv.shape[2]
    rows = NVIS * GI
    one = jax.ShapeDtypeStruct((rows, d), BF16)
    first = prev is None
    outs = [jax.ShapeDtypeStruct((3, 2, rows, hc), BF16), one, one]
    ins = [d_own, d_other] + ([] if first else list(prev)) + [qkv, w_qkv, w_proj]
    return pl.pallas_call(
        functools.partial(attn_bwd_kernel, first, rows),
        out_shape=outs,
        grid=(1,),
        in_specs=[whole(a.shape) for a in ins],
        out_specs=[whole(o.shape) for o in outs],
        scratch_shapes=[
            pltpu.VMEM((8, QPAD * GI, 128), F32),
            pltpu.VMEM((6, QPAD * GI, 128), F32),
        ],
        compiler_params=params(48),
        cost_estimate=cost(2 * 2 * rows * d * hc * 7, 10 * MIB),
        name="attn_bwd",
    )(*ins)


def join(pieces):
    return jnp.concatenate([p[...] for p in pieces], axis=1)


def mlp_kernel(a0, a1, p0, p1, p2, p3, w1, b1, w2, e0, e1, e2, e3, *outs):
    mlp0, mlp1, dh0, dh1, hid, dup, dmlp, gb = outs
    i = pl.program_id(0)
    a = jnp.where(i == 0, a0[...], a1[...])
    demb = jnp.concatenate([p0[0], p1[0], p2[0], p3[0]], axis=1)
    dm = dot(demb, join((e0, e1, e2, e3)), NT).astype(BF16)
    dmlp[0] = dm
    width = w1.shape[1]
    for f in range(0, width, 256):
        cols = slice(f, f + 256)
        up = dot(a, w1[:, cols]) + b1[:, cols]
        cdf = 0.5 * (1.0 + lax.erf(up * SQRT_HALF))
        hid[0, :, cols] = (up * cdf).astype(BF16)
        d_hid = dot(dm, w2[cols, :], NT)
        pdf = jnp.exp(up * up * -0.5) * INV_SQRT_2PI
        d_up = (d_hid * (cdf + up * pdf)).astype(BF16)
        dup[0, :, cols] = d_up
        s = jnp.sum(d_up.astype(F32), axis=0, keepdims=True)
        gb[:, cols] = jnp.where(i == 0, s, gb[:, cols] + s)
    dh = dot(dup[0], w1[...], NT).astype(BF16)
    mlp = dot(hid[0], w2[...]).astype(BF16)
    for r, (m_ref, d_ref) in enumerate(((mlp0, dh0), (mlp1, dh1))):

        @pl.when(i == r)
        def _():
            m_ref[...] = mlp
            d_ref[...] = dh


def mlp_pair(base, a_first, a_second, pieces, w1, b1, w2, we):
    rows, d = a_first.shape
    f = w1.shape[1]
    ec = pieces[0].shape[2]
    one = jax.ShapeDtypeStruct((rows, d), BF16)
    pair = jax.ShapeDtypeStruct((2, rows, d), BF16)
    hidden = jax.ShapeDtypeStruct((2, rows, f), BF16)
    step = lambda n: pl.BlockSpec((1, rows, n), lambda i: (i, 0, 0))
    piece = lambda r: pl.BlockSpec((1, rows, ec), lambda i: ((base + i) ^ r, 0, 0))
    return pl.pallas_call(
        mlp_kernel,
        out_shape=[one] * 4 + [hidden, hidden, pair, jax.ShapeDtypeStruct((1, f), F32)],
        grid=(2,),
        in_specs=[whole((rows, d))] * 2
        + [piece(r) for r in range(4)]
        + [whole(w1.shape), whole(b1.shape), whole(w2.shape)]
        + [whole(w.shape) for w in we],
        out_specs=[whole((rows, d))] * 4 + [step(f), step(f), step(d), whole((1, f))],
        compiler_params=params(48),
        cost_estimate=cost(2 * 2 * rows * d * f * 4.5, 18 * MIB, 4 * rows * f),
        name="mlp_pair",
    )(a_first, a_second, *pieces, w1, b1, w2, *we)


def own_rows(x_ref, c, k0, k1):
    lo, hi = image_rows(x_ref, k0, k1)
    return jnp.where(c == 0, lo, hi)


def ln2_kernel(meta, x_ref, keep, recv, g_ref, b_ref, x1_ref, a_ref, x_own):
    for k0 in range(0, NVIS, 7):
        sl = slice(k0 * GI, (k0 + 7) * GI)
        x = own_rows(x_ref, meta[1], k0, k0 + 7)
        x_own[sl, :] = x.astype(BF16)
        x1 = x + (
            keep[sl, :].astype(F32) + recv[sl, :].astype(F32)
        )
        x1_ref[sl, :] = x1
        a_ref[sl, :] = (normalize(x1)[0] * g_ref[...] + b_ref[...]).astype(BF16)


def ln2(meta, x3, part, recv, gain, shift):
    rows, d = recv.shape
    return pl.pallas_call(
        ln2_kernel,
        out_shape=[jax.ShapeDtypeStruct((rows, d), F32)] + [jax.ShapeDtypeStruct((rows, d), BF16)] * 2,
        grid_spec=pltpu.PrefetchScalarGridSpec(
            num_scalar_prefetch=1,
            grid=(1,),
            in_specs=[
                pl.BlockSpec((NVIS, 2 * GI, d), lambda i, m: (0, m[0], 0)),
                whole((rows, d)),
                whole((rows, d)),
                whole((1, d)),
                whole((1, d)),
            ],
            out_specs=[whole((rows, d))] * 3,
        ),
        compiler_params=params(32),
        cost_estimate=cost(20 * rows * d, 6 * MIB),
        name="ln2",
    )(meta, x3, part, recv, gain, shift)


def backward_rows(x, d_out, gain):
    xhat, inv = normalize(x)
    e = d_out * gain
    d_x = inv * (
        e
        - jnp.mean(e, axis=-1, keepdims=True)
        - xhat * jnp.mean(e * xhat, axis=-1, keepdims=True)
    )
    return d_x, jnp.sum(d_out * xhat, axis=0, keepdims=True), jnp.sum(d_out, axis=0, keepdims=True)


def ln2_bwd_kernel(
    x1, keep, r1, r2, p0, p1, p2, p3, e0, e1, e2, e3, g_ref, dx1, dattn, gg, gb
):
    rows = x1.shape[0]
    we = join((e0, e1, e2, e3))
    gg[...] = jnp.zeros_like(gg)
    gb[...] = jnp.zeros_like(gb)
    for r0 in range(0, rows, 56):
        sl = slice(r0, r0 + 56)
        demb = jnp.concatenate([p[0, sl, :] for p in (p0, p1, p2, p3)], axis=1)
        d_h = keep[sl, :].astype(F32) + r1[sl, :].astype(F32) + r2[sl, :].astype(F32)
        d_x, s_g, s_b = backward_rows(x1[sl, :], d_h, g_ref[...])
        d_x = d_x + dot(demb, we, NT)
        dx1[sl, :] = d_x
        dattn[sl, :] = d_x.astype(BF16)
        gg[...] += s_g
        gb[...] += s_b


def ln2_bwd(x1, dh2, r1, r2, pieces, we, gain):
    rows, d = x1.shape
    ec = pieces[0].shape[2]
    piece = lambda r: pl.BlockSpec((1, rows, ec), lambda i: (r, 0, 0))
    vec = jax.ShapeDtypeStruct((1, d), F32)
    return pl.pallas_call(
        ln2_bwd_kernel,
        out_shape=[
            jax.ShapeDtypeStruct((rows, d), F32),
            jax.ShapeDtypeStruct((rows, d), BF16),
            vec,
            vec,
        ],
        grid=(1,),
        in_specs=[
            whole((rows, d)),
            whole((rows, d)),
            whole((rows, d)),
            whole((rows, d)),
        ]
        + [piece(r) for r in range(4)]
        + [whole(w.shape) for w in we]
        + [whole((1, d))],
        out_specs=[whole((rows, d)), whole((rows, d)), whole((1, d)), whole((1, d))],
        compiler_params=params(32),
        cost_estimate=cost(2 * rows * d * DEC, 8 * MIB),
        name="ln2_bwd",
    )(x1, dh2, r1, r2, *pieces, *we, gain)


def ln1_bwd_kernel(meta, x_ref, dx1, keep, recv, g_ref, out, gg, gb):
    gg[...] = jnp.zeros_like(gg)
    gb[...] = jnp.zeros_like(gb)
    for k0 in range(0, NVIS, 7):
        sl = slice(k0 * GI, (k0 + 7) * GI)
        d_h = keep[sl, :].astype(F32) + recv[sl, :].astype(F32)
        d_x, s_g, s_b = backward_rows(own_rows(x_ref, meta[1], k0, k0 + 7), d_h, g_ref[...])
        out[sl, :] = (dx1[sl, :] + d_x).astype(BF16)
        gg[...] += s_g
        gb[...] += s_b


def ln1_bwd(meta, x3, dx1, dh1, recv, gain):
    rows, d = dx1.shape
    vec = jax.ShapeDtypeStruct((1, d), F32)
    return pl.pallas_call(
        ln1_bwd_kernel,
        out_shape=[jax.ShapeDtypeStruct((rows, d), BF16), vec, vec],
        grid_spec=pltpu.PrefetchScalarGridSpec(
            num_scalar_prefetch=1,
            grid=(1,),
            in_specs=[
                pl.BlockSpec((NVIS, 2 * GI, d), lambda i, m: (0, m[0], 0)),
                whole((rows, d)),
                whole((rows, d)),
                whole((rows, d)),
                whole((1, d)),
            ],
            out_specs=[whole((rows, d)), whole((1, d)), whole((1, d))],
        ),
        compiler_params=params(32),
        cost_estimate=cost(20 * rows * d, 6 * MIB),
        name="ln1_bwd",
    )(meta, x3, dx1, dh1, recv, gain)


def assemble_kernel(meta, g0, g1, g2, g3, out):
    i = pl.program_id(0)
    for r, g in enumerate((g0, g1, g2, g3)):

        @pl.when(i == r)
        def _():
            out[...] = g[...].astype(F32).reshape(out.shape)


def assemble(meta, groups):
    rows, d = groups[0].shape
    return pl.pallas_call(
        assemble_kernel,
        out_shape=jax.ShapeDtypeStruct((NVIS, 4 * GI, d), F32),
        grid_spec=pltpu.PrefetchScalarGridSpec(
            num_scalar_prefetch=1,
            grid=(4,),
            in_specs=[whole((rows, d))] * 4,
            out_specs=pl.BlockSpec((NVIS, GI, d), lambda i, m: (0, i ^ m[2], 0)),
        ),
        compiler_params=params(32),
        cost_estimate=cost(rows * d, 10 * MIB),
        name="assemble",
    )(meta, *groups)


def out_embed_kernel(x1, keep, r1, r2, e0, e1, e2, e3, z_ref, emb):
    mlp = keep[...].astype(F32) + r1[...].astype(F32) + r2[...].astype(F32)
    z = (x1[...] + mlp).astype(BF16)
    z_ref[...] = z
    e = dot(z, join((e0, e1, e2, e3))).astype(BF16)
    ec = emb.shape[2]
    for q in range(4):
        emb[q] = e[:, q * ec : (q + 1) * ec]


def out_embed(x1, mlp, r1, r2, we):
    rows, d = x1.shape
    ec = we[0].shape[1]
    return pl.pallas_call(
        out_embed_kernel,
        out_shape=[
            jax.ShapeDtypeStruct((rows, d), BF16),
            jax.ShapeDtypeStruct((4, rows, ec), BF16),
        ],
        grid=(1,),
        in_specs=[
            whole((rows, d)),
            whole((rows, d)),
            whole((rows, d)),
            whole((rows, d)),
        ]
        + [whole(w.shape) for w in we],
        out_specs=[whole((rows, d)), whole((4, rows, ec))],
        compiler_params=params(32),
        cost_estimate=cost(2 * rows * d * DEC, 6 * MIB),
        name="out_embed",
    )(x1, mlp, r1, r2, *we)


def collect_kernel(recv_index, cot, po, rows_out, token, csc):
    csc[...] = cot[...].astype(F32).reshape(csc.shape)
    total = jnp.sum(csc[...], axis=0, keepdims=True)
    if rows_out.shape[0] > cot.shape[1]:
        rows_out[...] = jnp.zeros_like(rows_out)
    images = cot.shape[1]
    lane = lax.broadcasted_iota(jnp.int32, (KPAD, GRID), 1)

    def image(g, seen):
        cells = csc[pl.ds(g, GRID, stride=images), :].astype(BF16)
        pick = jnp.where(po[g] == lane, 1.0, 0.0).astype(BF16)
        v = dot(pick, cells)
        rows_out[recv_index[g]] = v.astype(BF16)
        return seen + jnp.sum(v, axis=0, keepdims=True)

    seen = lax.fori_loop(0, images, image, jnp.zeros((1, 128), F32), unroll=4)
    token[...] = total - seen


def collect(recv_index, cot, po_cols, slots):
    return pl.pallas_call(
        collect_kernel,
        out_shape=[
            jax.ShapeDtypeStruct((slots, KPAD, 128), BF16),
            jax.ShapeDtypeStruct((1, 128), F32),
        ],
        grid_spec=pltpu.PrefetchScalarGridSpec(
            num_scalar_prefetch=1,
            grid=(1,),
            in_specs=[whole(cot.shape), whole(po_cols.shape)],
            out_specs=[whole((slots, KPAD, 128)), whole((1, 128))],
            scratch_shapes=[pltpu.VMEM((GRID * cot.shape[1], 128), F32)],
        ),
        compiler_params=params(32),
        cost_estimate=cost(2 * 32 * KPAD * GRID * 128, 4 * MIB),
        name="collect",
    )(recv_index, cot, po_cols)


def to_rows_kernel(meta, index, slots, out, sc):
    rows = out.shape[1]
    for s in range(4 * GI):
        v = slots[index[s]].astype(F32)
        sc[(s // GI) ^ meta[2], pl.ds(s % GI, KPAD, stride=GI), :] = v
    out[...] = sc[:, 0:rows, :].astype(BF16)


def to_rows(meta, index, slots):
    rows = NVIS * GI
    return pl.pallas_call(
        to_rows_kernel,
        out_shape=jax.ShapeDtypeStruct((4, rows, 128), BF16),
        grid_spec=pltpu.PrefetchScalarGridSpec(
            num_scalar_prefetch=2,
            grid=(1,),
            in_specs=[whole(slots.shape)],
            out_specs=whole((4, rows, 128)),
            scratch_shapes=[pltpu.VMEM((4, KPAD * GI, 128), F32)],
        ),
        compiler_params=params(16),
        cost_estimate=cost(4 * rows * 128, MIB),
        name="to_rows",
    )(meta, index, slots)


def to_slots_kernel(meta, index, e0, e1, e2, e3, out, sc):
    rows = e0.shape[-2]
    for r, e in enumerate((e0, e1, e2, e3)):
        sc[r, 0:rows, :] = e[...].reshape(rows, 128).astype(F32)
    sc[:, rows:, :] = jnp.zeros((4, KPAD * GI - rows, 128), F32)
    if out.shape[0] > 4 * GI:
        out[...] = jnp.zeros_like(out)
    for s in range(4 * GI):
        v = sc[(s // GI) ^ meta[2], pl.ds(s % GI, KPAD, stride=GI), :]
        out[index[s]] = v.astype(BF16)


def to_slots(meta, index, emb, received, slots):
    rows = NVIS * GI
    return pl.pallas_call(
        to_slots_kernel,
        out_shape=jax.ShapeDtypeStruct((slots, KPAD, 128), BF16),
        grid_spec=pltpu.PrefetchScalarGridSpec(
            num_scalar_prefetch=2,
            grid=(1,),
            in_specs=[pl.BlockSpec((1, rows, 128), lambda *_: (0, 0, 0))] + [whole((rows, 128))] * 3,
            out_specs=whole((slots, KPAD, 128)),
            scratch_shapes=[pltpu.VMEM((4, KPAD * GI, 128), F32)],
        ),
        compiler_params=params(16),
        cost_estimate=cost(4 * rows * 128, MIB),
        name="to_slots",
    )(meta, index, emb, *received)


def grid_kernel(meta, index, slots, po, token, table, out, sc):
    images = out.shape[1]
    cell = lax.broadcasted_iota(jnp.int32, (GRID, KPAD), 0)
    ones = jnp.ones((KPAD, 128), BF16)

    def image(g, carry):
        pick = jnp.where(po[g] == cell, 1.0, 0.0).astype(BF16)
        both = dot(pick, jnp.concatenate([slots[index[g]], ones], axis=1))
        v = jnp.where(both[:, 128:] > 0.5, both[:, :128], token[...])
        sc[pl.ds(g, GRID, stride=images), :] = v
        return carry

    lax.fori_loop(0, images, image, 0, unroll=4)

    def line(i, carry):
        for j in range(SIDE):
            u = jnp.where(meta[2] < 2, i, j)
            p = i * SIDE + j
            start = pl.multiple_of(p * images, images)
            out[p] = sc[pl.ds(start, images), :] + table[u]
        return carry

    lax.fori_loop(0, SIDE, line, 0)


def grid_out(meta, index, slots, po_rows, token, table):
    images = table.shape[1]
    return pl.pallas_call(
        grid_kernel,
        out_shape=jax.ShapeDtypeStruct((GRID, images, 128), F32),
        grid_spec=pltpu.PrefetchScalarGridSpec(
            num_scalar_prefetch=2,
            grid=(1,),
            in_specs=[whole(slots.shape), whole(po_rows.shape), whole((1, 128)), whole(table.shape)],
            out_specs=whole((GRID, images, 128)),
            scratch_shapes=[pltpu.VMEM((GRID * images, 128), F32)],
        ),
        compiler_params=params(32),
        cost_estimate=cost(2 * 32 * KPAD * GRID * 256, 5 * MIB),
        name="grid_out",
    )(meta, index, slots, po_rows, token, table)


def position_table(level_index, part):
    sample = GSD_LOW * jnp.exp(
        level_index.astype(F32) * (math.log(GSD_HIGH / GSD_LOW) / (GSD_LEVELS - 1))
    )
    quarter = DEC // 4
    angular = jnp.exp(jnp.arange(quarter).astype(F32) * (-math.log(10000.0) / quarter))
    coordinate = jnp.arange(SIDE).astype(F32)
    phase = sample[None, :, None] * (coordinate[:, None] * angular[None, :])[:, None, :]
    return jnp.where(part % 2 == 1, jnp.cos(phase), jnp.sin(phase))


def after(v, *others):
    return lax.optimization_barrier((v,) + others)[0]


def put_halves(swap, lo, hi, send, keep, at=()):
    send[(0, *at)] = jnp.where(swap, lo, hi).astype(BF16)
    keep[(0, *at)] = jnp.where(swap, hi, lo).astype(BF16)


def grad_kernel(split_rows, n, place, *refs):
    a_refs, b_refs, (send, keep) = refs[:n], refs[n : 2 * n], refs[2 * n :]
    total = None
    for a, b in zip(a_refs, b_refs):
        for g in range(a.shape[0]):
            t = dot(a[g], b[g], TN)
            total = t if total is None else total + t
    swap = place[0] == 1
    if split_rows:
        half = total.shape[0] // 2
        put_halves(swap, total[:half], total[half:], send, keep)
    else:
        half = total.shape[1] // 2
        put_halves(swap, total[:, :half], total[:, half:], send, keep)


def grad_weight(place, a_list, b_list, split_rows):
    rows = a_list[0].shape[1]
    m, n = a_list[0].shape[2], b_list[0].shape[2]
    if split_rows:
        a_spec = lambda g: pl.BlockSpec((g, rows, m // 4), lambda i, p: (0, 0, i))
        b_spec = lambda g: pl.BlockSpec((g, rows, n), lambda i, p: (0, 0, 0))
        shape = (4, m // 8, n)
    else:
        a_spec = lambda g: pl.BlockSpec((g, rows, m), lambda i, p: (0, 0, 0))
        b_spec = lambda g: pl.BlockSpec((g, rows, n // 4), lambda i, p: (0, 0, i))
        shape = (4, m, n // 8)
    return pl.pallas_call(
        functools.partial(grad_kernel, split_rows, len(a_list)),
        out_shape=[jax.ShapeDtypeStruct(shape, BF16)] * 2,
        grid_spec=pltpu.PrefetchScalarGridSpec(
            num_scalar_prefetch=1,
            grid=(4,),
            in_specs=[a_spec(a.shape[0]) for a in a_list] + [b_spec(b.shape[0]) for b in b_list],
            out_specs=[pl.BlockSpec((1,) + shape[1:], lambda i, p: (i ^ p[1], 0, 0))] * 2,
        ),
        compiler_params=params(48),
        cost_estimate=cost(2 * rows * m * n * sum(a.shape[0] for a in a_list), 8 * MIB),
        name="grad_weight",
    )(place, *a_list, *b_list)


def grad_qkv_kernel(place, a_ref, b_ref, send, keep):
    cols = b_ref.shape[3]
    swap = place[0] == 1
    for j in range(3):
        total = dot(a_ref[0], b_ref[j, 0], TN) + dot(a_ref[1], b_ref[j, 1], TN)
        half = total.shape[0] // 2
        put_halves(
            swap,
            total[:half],
            total[half:],
            send,
            keep,
            (slice(None), slice(j * cols, (j + 1) * cols)),
        )


def grad_qkv_weight(place, a, b):
    _, rows, m = a.shape
    cols = b.shape[3]
    shape = (4, m // 8, 3 * cols)
    return pl.pallas_call(
        grad_qkv_kernel,
        out_shape=[jax.ShapeDtypeStruct(shape, BF16)] * 2,
        grid_spec=pltpu.PrefetchScalarGridSpec(
            num_scalar_prefetch=1,
            grid=(4,),
            in_specs=[pl.BlockSpec((2, rows, m // 4), lambda i, p: (0, 0, i)), whole(b.shape)],
            out_specs=[pl.BlockSpec((1,) + shape[1:], lambda i, p: (i ^ p[1], 0, 0))] * 2,
        ),
        compiler_params=params(32),
        cost_estimate=cost(2 * 2 * rows * m * 3 * cols, 6 * MIB),
        name="grad_qkv",
    )(place, a, b)


MESH = pl.DeviceIdType.MESH
CHUNKS = [(0, 80), (80, 160), (160, 240), (240, 320), (320, 392)]


def flip(v, s):
    if s == 0:
        return v
    if s == 1:
        return v + 1 - 2 * lax.rem(v, 2)
    if s == 2:
        return lax.rem(v + 2, 4)
    return 3 - v


def add32(*refs):
    total = refs[0].astype(F32)
    for v in refs[1:]:
        total = total + v.astype(F32)
    return total


def main_kernel(names, *refs):
    r = types.SimpleNamespace(**dict(zip(names, refs)))
    d, t = lax.axis_index("dp"), lax.axis_index("tensor")
    x, z = lax.rem(d, 2), lax.div(d, 2)
    core, far = {"tensor": flip(t, 1)}, {"tensor": flip(t, 2)}
    beside = {"dp": d + 1 - 2 * x}
    along = [None] + [{"dp": 2 * flip(z, s) + x} for s in (1, 2, 3)]
    n_local, n_remote = itertools.count(), itertools.count()
    sent = []

    def fetch(src, dst):
        copy = pltpu.make_async_copy(src, dst, r.lsem.at[next(n_local)])
        copy.start()
        return copy

    def remote(src, dst, peer):
        n = next(n_remote)
        copy = pltpu.make_async_remote_copy(
            src_ref=src,
            dst_ref=dst,
            send_sem=r.ssem.at[n],
            recv_sem=r.rsem.at[n],
            device_id=peer,
            device_id_type=MESH,
        )
        sent.append(copy)
        return copy

    def send(src, dst, peer):
        copy = remote(src, dst, peer)
        copy.start()
        return copy

    def left(copy):
        copy.wait_send()
        sent[:] = [c for c in sent if c is not copy]

    ld_p = [fetch(getattr(r, f"p{k}"), r.P.at[k]) for k in range(4)]
    ld_we = [fetch(getattr(r, f"e{k}"), r.WE.at[:, 128 * k : 128 * (k + 1)]) for k in range(4)]
    ld_a2 = fetch(r.a2, r.A2.at[0])
    ld_w1 = fetch(r.w1, r.W1)
    ld_w2 = fetch(r.w2, r.W2)
    ld_x1 = fetch(r.x1, r.X1)
    ld_wp = [fetch(r.wpn, r.WP.at[0]), fetch(r.wpf, r.WP.at[1])]

    peers = [core, far, beside] + along[1:]
    barrier = pltpu.get_barrier_semaphore()
    for p in peers:
        pl.semaphore_signal(barrier, inc=1, device_id=p, device_id_type=MESH)
    pl.semaphore_wait(barrier, len(peers))

    a2_far = send(r.a2, r.A2.at[2], far)
    a2_core = send(r.a2, r.A2.at[1], core)
    a2_both = remote(r.A2.at[2], r.A2.at[3], core)
    dh_near = remote(r.DH.at[1], r.DHC.at[0], core)
    mlp_near = remote(r.MLP.at[1], r.MLPC.at[0], core)

    for c in ld_p + ld_we:
        c.wait()

    def d_mlp(g, carry):
        demb = jnp.concatenate([r.P[k, flip(g, k)] for k in range(4)], axis=1)
        r.DM[g] = dot(demb, r.WE[...], NT).astype(BF16)
        return carry

    lax.fori_loop(0, 4, d_mlp, 0)
    for c in (ld_a2, ld_w1, ld_w2):
        c.wait()

    def mlp(g, gb):
        @pl.when(g == 1)
        def _():
            a2_core.wait_recv()

        @pl.when(g == 2)
        def _():
            a2_far.wait_recv()
            a2_both.start()

        @pl.when(g == 3)
        def _():
            a2_both.wait_recv()

        a, dm = r.A2[g], r.DM[g]
        sums = []
        for f in range(0, r.W1.shape[1], 256):
            cols = slice(f, f + 256)
            up = dot(a, r.W1[:, cols]) + r.b1[:, cols]
            cdf = 0.5 * (1.0 + lax.erf(up * SQRT_HALF))
            r.HID[g, :, cols] = (up * cdf).astype(BF16)
            d_hid = dot(dm, r.W2[cols, :], NT)
            pdf = jnp.exp(up * up * -0.5) * INV_SQRT_2PI
            d_up = (d_hid * (cdf + up * pdf)).astype(BF16)
            r.DUP[g, :, cols] = d_up
            sums.append(jnp.sum(d_up.astype(F32), axis=0, keepdims=True))
        r.DH[g] = dot(r.DUP[g], r.W1[...], NT).astype(BF16)
        r.MLP[g] = dot(r.HID[g], r.W2[...]).astype(BF16)

        @pl.when(g == 1)
        def _():
            dh_near.start()
            mlp_near.start()

        return gb + jnp.concatenate(sums, axis=1)

    r.SM[4:5, :] = lax.fori_loop(0, 4, mlp, jnp.zeros((1, r.W1.shape[1]), F32))

    dh_far = send(r.DH.at[3], r.DHC.at[1], core)
    mlp_far = send(r.MLP.at[3], r.MLPC.at[1], core)
    dh_far.wait_recv()
    r.DH[2] = add32(r.DH[2], r.DHC[1]).astype(BF16)
    dh_y = send(r.DH.at[2], r.DHY, far)
    mlp_far.wait_recv()
    r.MLP[2] = add32(r.MLP[2], r.MLPC[1]).astype(BF16)
    mlp_y = send(r.MLP.at[2], r.MLPY, far)

    ld_wq = []
    for w_ref, w in ((r.W2, r.wqn), (r.W1, r.wqf)):
        ld_wq.append([fetch(w.at[j], w_ref.at[:, 256 * j : 256 * (j + 1)]) for j in range(3)])

    x_fc1 = []
    for i in range(4):
        total = None
        for g in range(4):
            v = dot(r.A2[g, :, 256 * i : 256 * (i + 1)], r.DUP[g], TN)
            total = v if total is None else total + v
        rel = flip(z, i)
        r.S1[rel] = jnp.where(x == 1, total[:128], total[128:]).astype(BF16)
        r.K1[rel] = jnp.where(x == 1, total[128:], total[:128]).astype(BF16)
        x_fc1.append(send(r.S1.at[rel], r.X1B.at[rel], beside))
    left(a2_both)
    left(a2_core)
    left(a2_far)
    ld_a1 = [fetch(r.a1.at[g], r.A2.at[g]) for g in range(2)]
    ld_att = [
        fetch(att.at[g], r.A2.at[2 + s, :, 256 * g : 256 * (g + 1)])
        for s, att in enumerate((r.attn, r.attf))
        for g in range(2)
    ]

    x_fc2 = []
    for m in range(4):
        total = None
        for g in range(4):
            v = dot(r.HID[g, :, 256 * m : 256 * (m + 1)], r.DM[g], TN)
            total = v if total is None else total + v
        for i in range(4):
            rel = flip(z, i)
            lo, hi = total[:, 256 * i : 256 * i + 128], total[:, 256 * i + 128 : 256 * (i + 1)]
            at = pl.ds(pl.multiple_of(rel * 128, 128), 128)
            at_keep = pl.ds(pl.multiple_of(512 + rel * 128, 128), 128)
            r.DUP[m, 0:256, at] = jnp.where(x == 1, lo, hi).astype(BF16)
            r.DUP[m, 0:256, at_keep] = jnp.where(x == 1, hi, lo).astype(BF16)
        x_fc2.append(send(r.DUP.at[m, 0:256, 0:512], r.X2B.at[m], beside))

    ld_qkv = [
        fetch(q.at[j, g], r.DM.at[2 * s + g, :, 256 * j : 256 * (j + 1)])
        for s, q in enumerate((r.qkvn, r.qkvf))
        for g in range(2)
        for j in range(3)
    ]

    dh_near.wait_recv()
    dh_y.wait_recv()
    ld_x1.wait()
    gg = gs = jnp.zeros((1, r.X1.shape[1]), F32)
    for a, b in CHUNKS:
        d_h = add32(r.DH[0, a:b], r.DHC[0, a:b], r.DHY[a:b])
        d_x, s_g, s_b = backward_rows(r.X1[a:b], d_h, r.g2[...])
        demb = jnp.concatenate([r.P[k, k, a:b] for k in range(4)], axis=1)
        d_x = d_x + dot(demb, r.WE[...], NT)
        r.DX1[a:b] = d_x
        r.DAT[0, a:b] = d_x.astype(BF16)
        gg, gs = gg + s_g, gs + s_b
    r.SM[2:3, :] = gg
    r.SM[3:4, :] = gs
    d_attn = send(r.DAT.at[0], r.DAT.at[1], core)

    for c in x_fc1:
        c.wait_recv()
    z_fc1 = []
    for s in (1, 2, 3):
        r.K1[s] = add32(r.K1[s], r.X1B[s]).astype(BF16)
        z_fc1.append(send(r.K1.at[s], r.Z1.at[s - 1], along[s]))

    for c in ld_wp + ld_att + ld_a1 + ld_wq[0] + ld_wq[1] + ld_qkv:
        c.wait()
    d_attn.wait_recv()

    x_proj = [None, None]
    for s in (1, 0):
        total = None
        for g in range(2):
            v = dot(r.A2[2 + s, :, 256 * g : 256 * (g + 1)], r.DAT[g], TN)
            total = v if total is None else total + v
        for i in range(4):
            rel = flip(z, i)
            lo, hi = total[:, 256 * i : 256 * i + 128], total[:, 256 * i + 128 : 256 * (i + 1)]
            r.SP[s, rel] = jnp.where(x == 1, lo, hi).astype(BF16)
            r.KP[s, rel] = jnp.where(x == 1, hi, lo).astype(BF16)
        x_proj[s] = send(r.SP.at[s], r.XP.at[s], beside)

    left(dh_near)
    masks = head_masks()
    rows = r.DAT.shape[1]
    r.SC[:, rows:, :] = jnp.zeros((8, r.SC.shape[1] - rows, 128), F32)

    def attention(s):
        wq = (r.W2, r.W1)[s]
        for g in (1, 0):
            for j in range(3):
                put_slabs(r.SC, j, rows, r.DM[2 * s + g, :, 256 * j : 256 * (j + 1)].astype(F32))
            put_slabs(r.SC, 3, rows, dot(r.DAT[g], r.WP[s], NT).astype(BF16).astype(F32))
            lax.fori_loop(
                0, GI, lambda i, c: attn_bwd_image(r.SC, r.DSC, masks, i, c), 0, unroll=4
            )
            total = r.DH[g].astype(F32) if s == 0 else None
            for j in range(3):
                d_j = jnp.concatenate(
                    [r.DSC[2 * j, 0:rows, :], r.DSC[2 * j + 1, 0:rows, :]], axis=1
                ).astype(BF16)
                r.HID[2 * s + g, :, 256 * j : 256 * (j + 1)] = d_j
                part = dot(d_j, wq[:, 256 * j : 256 * (j + 1)], NT)
                total = part if total is None else total + part
            r.DH[g] = total.astype(BF16)

    def grad_qkv(s):
        copies = []
        for i in range(4):
            total = None
            for g in range(2):
                v = dot(
                    r.A2[g, :, 256 * i : 256 * (i + 1)], r.HID[2 * s + g, :, 0:768], TN
                )
                total = v if total is None else total + v
            rel = flip(z, i)
            out = r.SQ.at[rel] if s == 0 else r.S1.at[rel, :, 0:768]
            out[...] = jnp.where(x == 1, total[:128], total[128:]).astype(BF16)
            r.KQ[s, rel] = jnp.where(x == 1, total[128:], total[:128]).astype(BF16)
            copies.append(send(out, r.XQ.at[s, rel], beside))
        return copies

    attention(1)
    for c in x_fc1:
        left(c)
    x_qkv = [None, grad_qkv(1)]

    for c in x_fc2:
        c.wait_recv()
    z_fc2 = []
    for s in (1, 2, 3):
        at = slice(512 + 128 * s, 640 + 128 * s)
        for m in range(4):
            got = r.X2B[m, :, 128 * s : 128 * (s + 1)]
            r.DUP[m, 0:256, at] = add32(r.DUP[m, 0:256, at], got).astype(BF16)
        z_fc2.append(send(r.DUP.at[:, 0:256, at], r.Z2.at[s - 1], along[s]))

    left(mlp_near)
    mlp_near.wait_recv()
    mlp_y.wait_recv()
    r.MLP[1] = (r.X1[...] + add32(r.MLP[0], r.MLPC[0], r.MLPY[...])).astype(BF16)
    emb = dot(r.MLP[1], r.WE[...]).astype(BF16)
    for q in range(4):
        r.EMB[q] = emb[:, 128 * q : 128 * (q + 1)]
    e_core = send(r.EMB.at[1], r.em1, core)
    e_y = send(r.EMB.at[2], r.em2, far)
    e_y2 = send(r.EMB.at[3], r.EF, far)
    ld_em = fetch(r.EMB.at[0], r.em0)
    ld_xo = fetch(r.xo, r.MLP.at[0])

    attention(0)
    dh1 = send(r.DH.at[1], r.DHC.at[1], core)
    x_qkv[0] = grad_qkv(0)

    z_proj = [[], []]
    for s in (1, 0):
        x_proj[s].wait_recv()
        for k in (1, 2, 3):
            r.KP[s, k] = add32(r.KP[s, k], r.XP[s, k]).astype(BF16)
            z_proj[s].append(send(r.KP.at[s, k], r.ZP.at[s, k - 1], along[k]))
    z_qkv = [[], []]

    def qkv_on(s):
        for c in x_qkv[s]:
            c.wait_recv()
        for k in (1, 2, 3):
            r.KQ[s, k] = add32(r.KQ[s, k], r.XQ[s, k]).astype(BF16)
            z_qkv[s].append(send(r.KQ.at[s, k], r.ZQ.at[s, k - 1], along[k]))

    left(mlp_y)
    ld_xo.wait()
    dh1.wait_recv()
    gg = gs = jnp.zeros((1, r.X1.shape[1]), F32)
    for a, b in CHUNKS:
        d_h = add32(r.DH[0, a:b], r.DHC[1, a:b])
        d_x, s_g, s_b = backward_rows(r.MLP[0, a:b].astype(F32), d_h, r.g1[...])
        r.MLP[2, a:b] = (r.DX1[a:b] + d_x).astype(BF16)
        gg, gs = gg + s_g, gs + s_b
    r.SM[0:1, :] = gg
    r.SM[1:2, :] = gs
    g_y = send(r.MLP.at[2], r.gi2, far)
    g_core = send(r.MLP.at[2], r.gi1, core)
    ld_gi = fetch(r.MLP.at[2], r.gi0)
    r.SM[5:6, :] = jnp.concatenate(
        [r.token[...], jnp.zeros((1, r.SM.shape[1] - 128), F32)], axis=1
    )
    r.SM[6:8, :] = jnp.zeros((2, r.SM.shape[1]), F32)
    sm_x = send(r.SM, r.SMR.at[0], beside)
    e_y2.wait_recv()
    e_both = send(r.EF, r.em3, core)

    demb = jnp.concatenate([r.P[k, k] for k in range(4)], axis=1)
    for i in range(4):
        total = dot(r.MLP[1, :, 256 * i : 256 * (i + 1)], demb, TN)
        rel = flip(z, i)
        for h, v in enumerate((total[:128], total[128:])):
            row = jnp.where(x == h, 1, 0)
            r.GE[row, rel] = jnp.concatenate([v[:, :128], v[:, 256:384]], axis=1).astype(BF16)
            r.GC[row, rel] = jnp.concatenate([v[:, 128:256], v[:, 384:]], axis=1).astype(BF16)
    ge_core = send(r.GC, r.GR, core)

    sm_x.wait_recv()
    r.SM2[...] = r.SM[...] + r.SMR[0]
    sm_z = [send(r.SM2, r.SMR.at[k], along[k]) for k in (1, 2, 3)]

    ge_core.wait_recv()
    r.GE[...] = add32(r.GE[...], r.GR[...]).astype(BF16)
    ge_x = send(r.GE.at[0], r.XE, beside)
    qkv_on(1)
    for c in sm_z:
        c.wait_recv()
    r.SM3[...] = r.SM2[...] + r.SMR[1] + r.SMR[2] + r.SMR[3]
    sm_core = send(r.SM3, r.SMR.at[4], core)
    ge_x.wait_recv()
    z_ge = []
    for k in (1, 2, 3):
        r.GE[1, k] = add32(r.GE[1, k], r.XE[k]).astype(BF16)
        z_ge.append(send(r.GE.at[1, k], r.ZE.at[k - 1], along[k]))
    qkv_on(0)
    sm_core.wait_recv()
    r.SM4[...] = r.SM3[...] + r.SMR[4]
    sm_y = send(r.SM4, r.SMR.at[5], far)

    for c in z_fc1 + z_fc2 + z_proj[1] + z_proj[0]:
        c.wait_recv()
    r.o_fc1[...] = add32(r.K1[0], r.X1B[0], r.Z1[0], r.Z1[1], r.Z1[2])
    for m in range(4):
        r.o_fc2[256 * m : 256 * (m + 1), :] = add32(
            r.DUP[m, 0:256, 512:640], r.X2B[m, :, 0:128], r.Z2[0, m], r.Z2[1, m], r.Z2[2, m]
        )
    r.FP[...] = add32(r.KP[1, 0], r.XP[1, 0], r.ZP[1, 0], r.ZP[1, 1], r.ZP[1, 2]).astype(BF16)
    y_proj = send(r.FP, r.YP, far)
    g_y.wait_recv()
    g_both = send(r.gi2, r.gi3, core)
    for c in z_qkv[1]:
        c.wait_recv()
    r.FQ[...] = add32(r.KQ[1, 0], r.XQ[1, 0], r.ZQ[1, 0], r.ZQ[1, 1], r.ZQ[1, 2]).astype(BF16)
    y_qkv = send(r.FQ, r.YQ, far)
    for c in z_ge:
        c.wait_recv()
    two = add32(r.GE[1, 0], r.XE[0], r.ZE[0], r.ZE[1], r.ZE[2])
    r.FE[...] = two[:, 128:].astype(BF16)
    y_emb = send(r.FE, r.YE, far)
    for c in z_qkv[0]:
        c.wait_recv()
    own = add32(r.KQ[0, 0], r.XQ[0, 0], r.ZQ[0, 0], r.ZQ[0, 1], r.ZQ[0, 2])
    y_qkv.wait_recv()
    own = own + r.YQ[...].astype(F32)
    for j in range(3):
        r.o_qkv[j] = own[:, 256 * j : 256 * (j + 1)]
    y_proj.wait_recv()
    r.o_proj[...] = add32(
        r.KP[0, 0], r.XP[0, 0], r.ZP[0, 0], r.ZP[0, 1], r.ZP[0, 2], r.YP[...]
    )
    y_emb.wait_recv()
    r.o_emb[...] = two[:, :128] + r.YE[...].astype(F32)
    sm_y.wait_recv()
    r.o_sum[0:4] = r.SM4[0:4] + r.SMR[5, 0:4]
    r.o_sum[4:8] = r.SM3[4:8]
    g_core.wait_recv()
    g_both.wait_recv()
    e_core.wait_recv()
    e_y.wait_recv()
    e_both.wait_recv()
    for c in (ld_em, ld_gi):
        c.wait()
    for c in sent:
        c.wait_send()


def main_call(ins, g1, g2, b1, token):
    rows, width = ins["a2"].shape
    bf = lambda *s: jax.ShapeDtypeStruct(s, BF16)
    f32 = lambda *s: jax.ShapeDtypeStruct(s, F32)
    vm = lambda *s: pltpu.VMEM(s, BF16)
    vf = lambda *s: pltpu.VMEM(s, F32)
    small = dict(g1=g1, g2=g2, b1=b1, token=token)
    outs = {f"gi{k}": bf(rows, width) for k in range(4)}
    outs |= {f"em{k}": bf(rows, 128) for k in range(4)}
    dense = dict(
        o_fc1=f32(128, width),
        o_fc2=f32(width, 128),
        o_proj=f32(256, 128),
        o_qkv=f32(3, 128, 256),
        o_emb=f32(128, 128),
        o_sum=f32(8, width),
    )
    scratch = dict(
        P=vm(4, 4, rows, 128),
        WE=vm(width, 512),
        W1=vm(width, width),
        W2=vm(width, width),
        WP=vm(2, 256, width),
        A2=vm(4, rows, width),
        HID=vm(4, rows, width),
        DUP=vm(4, rows, width),
        DM=vm(4, rows, width),
        DH=vm(4, rows, width),
        MLP=vm(4, rows, width),
        DHC=vm(2, rows, width),
        MLPC=vm(2, rows, width),
        DHY=vm(rows, width),
        MLPY=vm(rows, width),
        X1=vf(rows, width),
        DX1=vf(rows, width),
        DAT=vm(2, rows, width),
        SC=vf(8, QPAD * GI, 128),
        DSC=vf(6, QPAD * GI, 128),
        S1=vm(4, 128, width),
        K1=vm(4, 128, width),
        X1B=vm(4, 128, width),
        Z1=vm(3, 128, width),
        X2B=vm(4, 256, 512),
        Z2=vm(3, 4, 256, 128),
        SP=vm(2, 4, 256, 128),
        KP=vm(2, 4, 256, 128),
        XP=vm(2, 4, 256, 128),
        ZP=vm(2, 3, 256, 128),
        FP=vm(256, 128),
        YP=vm(256, 128),
        SQ=vm(4, 128, 768),
        KQ=vm(2, 4, 128, 768),
        XQ=vm(2, 4, 128, 768),
        ZQ=vm(2, 3, 128, 768),
        FQ=vm(128, 768),
        YQ=vm(128, 768),
        EMB=vm(4, rows, 128),
        EF=vm(rows, 128),
        GE=vm(2, 4, 128, 256),
        GC=vm(2, 4, 128, 256),
        GR=vm(2, 4, 128, 256),
        XE=vm(4, 128, 256),
        ZE=vm(3, 128, 256),
        FE=vm(128, 128),
        YE=vm(128, 128),
        SM=vf(8, width),
        SM2=vf(8, width),
        SM3=vf(8, width),
        SM4=vf(8, width),
        SMR=vf(6, 8, width),
        lsem=pltpu.SemaphoreType.DMA((64,)),
        ssem=pltpu.SemaphoreType.DMA((96,)),
        rsem=pltpu.SemaphoreType.DMA((96,)),
    )
    names = list(ins) + list(small) + list(outs) + list(dense) + list(scratch)
    anywhere = pl.BlockSpec(memory_space=pl.ANY)
    in_vmem = pl.BlockSpec(memory_space=pltpu.VMEM)
    res = pl.pallas_call(
        functools.partial(main_kernel, names),
        out_shape=list(outs.values()) + list(dense.values()),
        in_specs=[anywhere] * len(ins) + [in_vmem] * len(small),
        out_specs=[anywhere] * len(outs) + [in_vmem] * len(dense),
        scratch_shapes=list(scratch.values()),
        compiler_params=pltpu.CompilerParams(
            vmem_limit_bytes=63 * MIB, collective_id=0, has_side_effects=True
        ),
        cost_estimate=cost(2e10, 50 * MIB),
        name="layer_main",
    )(*ins.values(), *small.values())
    return types.SimpleNamespace(**dict(zip(list(outs) + list(dense), res)))


def local(
    encoder_input,
    ln1_gain,
    ln1_bias,
    qkv_weight,
    proj_weight,
    ln2_gain,
    ln2_bias,
    fc1_weight,
    fc1_bias,
    fc2_weight,
    embed_weight,
    mask_token,
    grid_cotangent,
    image_order,
    patch_order,
    gsd_index,
):
    ndp = lax.axis_size("dp")
    d = lax.axis_index("dp")
    t = lax.axis_index("tensor")
    images, _, width = encoder_input.shape
    rows = NVIS * GI
    xbit, zpos = d % 2, d // 2
    meta = jnp.stack([t // 2, t % 2, t]).astype(jnp.int32)

    def over_core(v):
        return lax.ppermute(v, "tensor", [(i, i ^ 1) for i in range(4)])

    def over_y(v):
        return lax.ppermute(v, "tensor", [(i, i ^ 2) for i in range(4)])

    def over_x(v):
        return lax.ppermute(v, "dp", [(i, i ^ 1) for i in range(ndp)])

    pick = functools.partial(lax.dynamic_index_in_dim, axis=0, keepdims=False)

    g1 = ln1_gain.astype(F32)[None, :]
    s1 = ln1_bias.astype(F32)[None, :]
    g2 = ln2_gain.astype(F32)[None, :]
    s2 = ln2_bias.astype(F32)[None, :]
    bias_up = fc1_bias.astype(F32)[None, :]
    x3 = encoder_input.transpose(1, 0, 2)
    cot = grid_cotangent.transpose(1, 0, 2)
    w_qkv = qkv_weight.transpose(1, 0, 2)

    def y_half(w, axis):
        half = w.shape[axis] // 2
        return over_y(lax.dynamic_slice_in_dim(w, xbit * half, half, axis))

    def both_halves(mine, axis):
        other = over_x(mine)
        lo = jnp.where(xbit == 0, mine, other)
        hi = jnp.where(xbit == 0, other, mine)
        return jnp.concatenate([lo, hi], axis=axis)

    half_qk = y_half(w_qkv[:2], 1)
    half_v = y_half(w_qkv[2:], 1)
    half_proj = y_half(proj_weight, 0)
    we_core = over_core(embed_weight)
    we_y = over_y(embed_weight)

    capacity = max(1, images // ndp)
    slots = ndp * capacity
    own_images = lax.dynamic_slice_in_dim(image_order, d * images, images)
    dest = own_images // images
    before = jnp.arange(images)[None, :] < jnp.arange(images)[:, None]
    rank = jnp.sum((dest[:, None] == dest[None, :]) & before, axis=1)
    send_index = (dest * capacity + rank).astype(jnp.int32)
    every = jnp.arange(image_order.shape[0])
    wanted = d * images + jnp.arange(images)
    slot = jnp.sum(jnp.where(image_order[None, :] == wanted[:, None], every[None, :], 0), axis=1)
    source = slot // images
    to_me = image_order // images == d
    earlier = (
        to_me[None, :]
        & (every[None, :] // images == source[:, None])
        & (every[None, :] < slot[:, None])
    )
    recv_index = (source * capacity + jnp.sum(earlier, axis=1)).astype(jnp.int32)

    visible = jnp.pad(
        patch_order[:, :NVIS], ((0, 0), (0, KPAD - NVIS)), constant_values=-1
    )

    def over_dp(v):
        return lax.all_to_all(v, "dp", split_axis=0, concat_axis=0, tiled=True)

    back, token_grad = collect(recv_index, cot, visible[:, :, None], slots)
    back = over_dp(back)
    p0 = to_rows(meta, send_index, back)
    p1, p2 = over_core(p0), over_y(p0)

    w_qk_far = both_halves(half_qk, 1)
    g1_later = after(g1, half_qk, p0)
    a1, qkv_a, att_a, own_a, other_a = attn_fwd(
        meta, True, [x3, g1_later, s1], w_qkv, proj_weight
    )
    half_v, half_proj = after(half_v, a1), after(half_proj, a1)
    w_qkv_far = jnp.concatenate([w_qk_far, both_halves(half_v, 1)], axis=0)
    w_proj_far = both_halves(half_proj, 0)
    we_y, p2 = after(we_y, a1), after(p2, a1)
    we = (embed_weight, we_core, we_y, over_core(we_y))
    p3 = over_core(p2)
    pieces = (p0, p1, p2, p3)
    table = position_table(gsd_index, t)
    qkv_b, att_b, own_b, other_b = attn_fwd(
        meta, False, [after(a1, table), own_a, other_a], w_qkv_far, w_proj_far
    )
    x1, a2, x_own = ln2(meta, x3, own_b, over_core(other_b), g2, s2)
    if ndp == 8:
        main = main_call(
            dict(
                zip(["p0", "p1", "p2", "p3"], pieces),
                **dict(zip(["e0", "e1", "e2", "e3"], we)),
                a2=a2,
                x1=x1,
                xo=x_own,
                w1=fc1_weight,
                w2=fc2_weight,
                wpn=proj_weight,
                wpf=w_proj_far,
                wqn=w_qkv,
                wqf=w_qkv_far,
                a1=a1,
                attn=att_a,
                attf=att_b,
                qkvn=qkv_a,
                qkvf=qkv_b,
            ),
            g1,
            g2,
            bias_up,
            token_grad,
        )
        sent = to_slots(meta, send_index, main.em0[None], (main.em1, main.em2, main.em3), slots)
        grid_features = grid_out(
            meta,
            recv_index,
            over_dp(sent),
            visible[:, None, :],
            mask_token.astype(F32)[None, :],
            table,
        )
        grad_input = assemble(meta, (main.gi0, main.gi1, main.gi2, main.gi3))
        return (
            grid_features.transpose(1, 0, 2),
            grad_input.transpose(1, 0, 2),
            main.o_sum[0],
            main.o_sum[1],
            main.o_qkv.transpose(1, 0, 2),
            main.o_proj,
            main.o_sum[2],
            main.o_sum[3],
            main.o_fc1,
            main.o_sum[4],
            main.o_fc2,
            main.o_emb,
            main.o_sum[5, :128],
        )

    a2_y = over_y(a2)
    a2_core = over_core(a2)

    mlp0, mlp1, dh0, dh1, hid_n, dup_n, dm_n, gb_n = mlp_pair(
        0, a2, a2_core, pieces, fc1_weight, bias_up, fc2_weight, we
    )
    dh_core, mlp_core = over_core(dh1), over_core(mlp1)
    a2_y = after(a2_y, dh0)
    a2_far = over_core(a2_y)
    mlp2, mlp3, dh2, dh3, hid_f, dup_f, dm_f, gb_f = mlp_pair(
        2, a2_y, a2_far, pieces, fc1_weight, bias_up, fc2_weight, we
    )

    def add16(a, b):
        return (a.astype(F32) + b.astype(F32)).astype(BF16)

    fast = ndp == 8
    place = jnp.stack([xbit, zpos]).astype(jnp.int32) if fast else jnp.zeros((2,), jnp.int32)

    def stage_x(parts):
        send, keep = parts
        return keep, over_x(send) if fast else send

    def stage_z(held, *done):
        if not fast:
            return held
        keep, got = held
        got = after(got, *done)
        arrived = [
            lax.ppermute(add16(keep[s], got[s]), "dp", [(i, i ^ (2 * s)) for i in range(8)])
            for s in range(1, 4)
        ]
        return keep[0].astype(F32) + got[0].astype(F32), arrived

    def stage_sum(held, axis, *done):
        if not fast:
            flat = jnp.stack(held, axis=1)
            if axis == 1:
                flat = flat.transpose(2, 0, 1, 3)
                flat = flat.reshape(flat.shape[0], -1)
            else:
                flat = flat.reshape(-1, flat.shape[-1])
            return lax.psum_scatter(flat, "dp", scatter_dimension=axis, tiled=True).astype(F32)
        total, arrived = held
        for v in after(tuple(arrived), *done):
            total = total + v.astype(F32)
        return total

    def pairs(v):
        return [v[0:1], v[1:2]]

    dh_sum = add16(dh2, over_core(dh3))
    dh_y = over_y(dh_sum)
    fc2_w = grad_weight(place, [after(hid_n, dh_sum), hid_f], [dm_n, dm_f], False)
    fc2_x = stage_x(fc2_w)
    mlp_sum = add16(after(mlp2, fc2_w[0]), over_core(mlp3))
    mlp_y = over_y(mlp_sum)
    a2_parts = [after(a2, mlp_sum)[None], a2_core[None], a2_y[None], a2_far[None]]
    fc1_w = grad_weight(place, a2_parts, pairs(dup_n) + pairs(dup_f), True)
    fc1_x = stage_x(fc1_w)

    dx1, d_attn, gg2, gs2 = ln2_bwd(x1, after(dh0, fc1_w[0]), dh_core, dh_y, pieces, we, g2)
    d_attn_core = over_core(d_attn)
    d_pair = [d_attn[None], d_attn_core[None]]
    proj_far_w = grad_weight(place, pairs(att_b), d_pair, False)
    proj_far_x = stage_x(proj_far_w)
    proj_near_w = grad_weight(place, pairs(after(att_a, proj_far_w[0])), d_pair, False)
    proj_near_x = stage_x(proj_near_w)
    dqkv_b, own_b, other_b = attn_bwd(
        after(d_attn, proj_near_w[0]), d_attn_core, None, qkv_b, w_qkv_far, w_proj_far
    )
    qkv_far_w = grad_qkv_weight(place, a1, dqkv_b)
    qkv_far_x = stage_x(qkv_far_w)
    fc2_z = stage_z(fc2_x, qkv_far_w[0])
    z, emb = out_embed(after(x1, fc2_z[0]), mlp0, mlp_core, mlp_y, we)
    e_core, e2 = over_core(emb[1]), over_y(emb[2:4])
    dqkv_a, own_a, other_a = attn_bwd(
        after(d_attn, z), d_attn_core, (own_b, other_b), qkv_a, w_qkv, proj_weight
    )
    dh1_core = over_core(other_a)
    qkv_near_w = grad_qkv_weight(place, a1, dqkv_a)
    qkv_near_x = stage_x(qkv_near_w)
    fc1_z = stage_z(fc1_x, qkv_near_w[0])
    g_own, gg1, gs1 = ln1_bwd(meta, x3, after(dx1, fc1_z[0]), own_a, dh1_core, g1)
    g_y = over_y(g_own)
    g_core = over_core(g_own)
    small = jnp.concatenate(
        [gg1, gs1, gg2, gs2, gb_n + gb_f, jnp.pad(token_grad, ((0, 0), (0, width - 128)))], axis=0
    )
    step = 1
    while step < ndp:
        small = small + lax.ppermute(small, "dp", [(i, i ^ step) for i in range(ndp)])
        step *= 2
    sums = small[:4] + over_core(small[:4])
    sums = sums + over_y(sums)
    gb, token_sum = small[4:5], small[5:6, :128]

    e2 = after(e2, g_own)
    sent = to_slots(meta, send_index, emb, (e_core, e2[0], over_core(e2[1])), slots)
    arrived = over_dp(sent)
    qkv_far_z = stage_z(qkv_far_x, arrived)
    proj_far_z = stage_z(proj_far_x, arrived)
    proj_near_z = stage_z(proj_near_x, arrived)
    demb_own = jnp.concatenate([p[r : r + 1] for r, p in enumerate(pieces)], axis=2)
    ec = embed_weight.shape[1]
    embed_w = grad_weight(place, [after(z, arrived)[None]], [demb_own], True)
    embed_w = [
        add16(
            jnp.concatenate([v[..., :ec], v[..., 2 * ec : 3 * ec]], axis=-1),
            over_core(jnp.concatenate([v[..., ec : 2 * ec], v[..., 3 * ec :]], axis=-1)),
        )
        for v in embed_w
    ]
    embed_x = stage_x(embed_w)
    grid_features = grid_out(
        meta,
        recv_index,
        after(arrived, embed_w[0]),
        visible[:, None, :],
        mask_token.astype(F32)[None, :],
        table,
    )
    qkv_near_z = stage_z(qkv_near_x, grid_features)
    embed_z = stage_z(embed_x, grid_features)

    def over_pair(near, far):
        return near + over_y(far.astype(BF16)).astype(F32)

    grad_fc2 = stage_sum(fc2_z, 1, grid_features)
    grad_fc1 = stage_sum(fc1_z, 0, grid_features)
    grad_proj = over_pair(
        stage_sum(proj_near_z, 1, grid_features), stage_sum(proj_far_z, 1, grid_features)
    )
    grad_qkv = over_pair(
        stage_sum(qkv_near_z, 0, grid_features), stage_sum(qkv_far_z, 0, grid_features)
    )
    hc = qkv_weight.shape[2]
    grad_qkv = jnp.stack([grad_qkv[:, j * hc : (j + 1) * hc] for j in range(3)], axis=1)
    embed_two = stage_sum(embed_z, 0)
    grad_embed = over_pair(embed_two[:, :ec], embed_two[:, ec:])
    grad_input = assemble(meta, (g_own, g_core, g_y, over_core(g_y)))
    return (
        grid_features.transpose(1, 0, 2),
        grad_input.transpose(1, 0, 2),
        sums[0],
        sums[1],
        grad_qkv,
        grad_proj,
        sums[2],
        sums[3],
        grad_fc1,
        gb[0],
        grad_fc2,
        grad_embed,
        token_sum[0],
    )


def solution(mesh):
    return jax.shard_map(
        local,
        mesh=mesh,
        in_specs=(
            P("dp", None, None),
            P(),
            P(),
            P(None, None, "tensor"),
            P("tensor", None),
            P(),
            P(),
            P(None, "tensor"),
            P("tensor"),
            P("tensor", None),
            P(None, "tensor"),
            P("tensor"),
            P("dp", None, "tensor"),
            P(),
            P("dp", None),
            P("dp"),
        ),
        out_specs=(
            P("dp", None, "tensor"),
            P("dp", None, None),
            P(),
            P(),
            P("dp", None, "tensor"),
            P("tensor", "dp"),
            P(),
            P(),
            P("dp", "tensor"),
            P("tensor"),
            P("tensor", "dp"),
            P("dp", "tensor"),
            P("tensor"),
        ),
        check_vma=False,
    )
```

```python
import functools
import itertools
import math
import types

import jax
import jax.numpy as jnp
from jax import lax
from jax.experimental import pallas as pl
from jax.experimental.pallas import tpu as pltpu
from jax.sharding import PartitionSpec as P

HEAD_DIM = 64
DEC = 512
SIDE = 14
GSD_LEVELS = 16
GRID = 196
NVIS = 49
KPAD = 56
QPAD = 64
GI = 8
EPS = 1e-06
GSD_LOW = 0.3
GSD_HIGH = 10.0
F32 = jnp.float32
BF16 = jnp.bfloat16
SCALE = HEAD_DIM ** (-0.5)
SQRT_HALF = math.sqrt(0.5)
INV_SQRT_2PI = 1.0 / math.sqrt(2.0 * math.pi)
MIB = 1024 * 1024

NT = (((1,), (1,)), ((), ()))
NN = (((1,), (0,)), ((), ()))
TN = (((0,), (0,)), ((), ()))


def dot(a, b, dims=NN):
    return lax.dot_general(a, b, dims, preferred_element_type=F32)


def params(vmem, steps=1):
    if lax.axis_size("dp") != 8:
        vmem = 56
    return pltpu.CompilerParams(
        vmem_limit_bytes=vmem * MIB, dimension_semantics=("arbitrary",) * steps
    )


def cost(flops, nbytes, trans=0):
    return pl.CostEstimate(flops=int(flops), bytes_accessed=int(nbytes), transcendentals=int(trans))


def whole(shape):
    return pl.BlockSpec(shape, lambda *_: (0,) * len(shape))


def normalize(x):
    mean = jnp.mean(x, axis=-1, keepdims=True)
    centred = x - mean
    inv = lax.rsqrt(jnp.mean(centred * centred, axis=-1, keepdims=True) + EPS)
    return centred * inv, inv


def image_rows(x_ref, k0, k1):
    x = x_ref[k0:k1].astype(F32)
    n, _, d = x.shape
    return x[:, :GI].reshape(n * GI, d), x[:, GI:].reshape(n * GI, d)


def head_masks():
    lane = lax.broadcasted_iota(jnp.int32, (1, 4 * HEAD_DIM), 1) // HEAD_DIM
    return [lane == h for h in range(4)]


def stack_heads(v, masks):
    return jnp.concatenate([jnp.where(m, v, 0.0) for m in masks], axis=0).astype(BF16)


def fold_heads(v, masks):
    out = jnp.where(masks[0], v[:QPAD], 0.0)
    for h in range(1, 4):
        out = out + jnp.where(masks[h], v[h * QPAD : (h + 1) * QPAD], 0.0)
    return out


def load_image(ref, j, s, rows):
    return jnp.concatenate(
        [ref[2 * j + l, pl.ds(s, rows, stride=GI), :] for l in range(2)], axis=1
    )


def store_image(ref, j, s, rows, v):
    for l in range(2):
        ref[2 * j + l, pl.ds(s, rows, stride=GI), :] = v[:rows, 128 * l : 128 * (l + 1)]


def softmax_t(keys, stacked):
    st = dot(keys, stacked, NT)
    row = lax.broadcasted_iota(jnp.int32, st.shape, 0)
    st = jnp.where(row < NVIS, st, -1e30)
    e = jnp.exp(st - jnp.max(st, axis=0, keepdims=True))
    return e * (1.0 / jnp.sum(e, axis=0, keepdims=True))


def put_slabs(ref, j, rows, v):
    for l in range(2):
        ref[2 * j + l, 0:rows, :] = v[:, 128 * l : 128 * (l + 1)]


def attn_fwd_kernel(first, rows, meta, *refs):
    if first:
        x_ref, g_ref, b_ref, wq_ref, wp_ref, a_ref, qkv_ref, att_ref, own_ref, other_ref, sc, osc = refs
        c = meta[1]
        for k0 in range(0, NVIS, 7):
            lo, hi = image_rows(x_ref, k0, k0 + 7)
            own, other = jnp.where(c == 0, lo, hi), jnp.where(c == 0, hi, lo)
            for g, v in enumerate((own, other)):
                a_ref[g, k0 * GI : (k0 + 7) * GI, :] = (
                    normalize(v)[0] * g_ref[...] + b_ref[...]
                ).astype(BF16)
    else:
        a_ref, prev0, prev1, wq_ref, wp_ref, qkv_ref, att_ref, own_ref, other_ref, sc, osc = refs
    sc[:, rows:, :] = jnp.zeros((6, sc.shape[1] - rows, 128), F32)
    masks = head_masks()
    for g in (1, 0):
        a = a_ref[g]
        for j in range(3):
            v = dot(a, wq_ref[j]).astype(BF16)
            qkv_ref[j, g] = v
            put_slabs(sc, j, rows, v.astype(F32))

        def image(s, carry):
            q = load_image(sc, 0, s, QPAD) * SCALE
            k = load_image(sc, 1, s, KPAD).astype(BF16)
            v = load_image(sc, 2, s, KPAD).astype(BF16)
            probs = softmax_t(k, stack_heads(q, masks))
            out = dot(probs.T.astype(BF16), v)
            store_image(osc, 0, s, QPAD, fold_heads(out, masks))
            return carry

        lax.fori_loop(0, GI, image, 0, unroll=True)
        att = jnp.concatenate([osc[0, 0:rows, :], osc[1, 0:rows, :]], axis=1).astype(BF16)
        att_ref[g] = att
        part = dot(att, wp_ref[...])
        if not first:
            part = part + (prev0, prev1)[g][...].astype(F32)
        (own_ref, other_ref)[g][...] = part.astype(BF16)


def attn_fwd(meta, first, ins, w_qkv, w_proj):
    d = w_qkv.shape[1]
    hc = w_qkv.shape[2]
    rows = NVIS * GI
    pair = jax.ShapeDtypeStruct((2, rows, d), BF16)
    outs = [
        jax.ShapeDtypeStruct((3, 2, rows, hc), BF16),
        jax.ShapeDtypeStruct((2, rows, hc), BF16),
        jax.ShapeDtypeStruct((rows, d), BF16),
        jax.ShapeDtypeStruct((rows, d), BF16),
    ]
    if first:
        outs = [pair] + outs
        specs = [
            pl.BlockSpec((NVIS, 2 * GI, d), lambda i, m: (0, m[0], 0)),
            whole((1, d)),
            whole((1, d)),
        ]
    else:
        specs = [whole((2, rows, d)), whole((rows, d)), whole((rows, d))]
    specs += [whole((3, d, hc)), whole((hc, d))]
    return pl.pallas_call(
        functools.partial(attn_fwd_kernel, first, rows),
        out_shape=outs,
        grid_spec=pltpu.PrefetchScalarGridSpec(
            num_scalar_prefetch=1,
            grid=(1,),
            in_specs=specs,
            out_specs=[whole(o.shape) for o in outs],
            scratch_shapes=[
                pltpu.VMEM((6, QPAD * GI, 128), F32),
                pltpu.VMEM((2, QPAD * GI, 128), F32),
            ],
        ),
        compiler_params=params(48),
        cost_estimate=cost(2 * 2 * rows * d * hc * 6, 10 * MIB),
        name="attn_fwd",
    )(meta, *ins, w_qkv, w_proj)


def attn_bwd_image(sc, dsc, masks, s, carry):
    q = stack_heads(load_image(sc, 0, s, QPAD) * SCALE, masks)
    k = load_image(sc, 1, s, KPAD).astype(BF16)
    v = load_image(sc, 2, s, KPAD).astype(BF16)
    dh = stack_heads(load_image(sc, 3, s, QPAD), masks)
    probs = softmax_t(k, q)
    d_probs = dot(v, dh, NT)
    d_v = dot(probs.astype(BF16), dh)
    total = jnp.sum(d_probs * probs, axis=0, keepdims=True)
    d_scores = probs * (d_probs - total)
    d_k = dot(d_scores.astype(BF16), q)
    d_q = fold_heads(dot(d_scores.T.astype(BF16), k), masks) * SCALE
    store_image(dsc, 0, s, QPAD, d_q)
    store_image(dsc, 1, s, KPAD, d_k)
    store_image(dsc, 2, s, KPAD, d_v)
    return carry


def attn_bwd_kernel(first, rows, *refs):
    if first:
        d0_ref, d1_ref, qkv_ref, wq_ref, wp_ref, dqkv_ref, own_ref, other_ref, sc, dsc = refs
    else:
        (
            d0_ref, d1_ref, prev0, prev1, qkv_ref, wq_ref, wp_ref,
            dqkv_ref, own_ref, other_ref, sc, dsc,
        ) = refs
    sc[:, rows:, :] = jnp.zeros((8, sc.shape[1] - rows, 128), F32)
    masks = head_masks()
    for g in (1, 0):
        d_attn = (d0_ref, d1_ref)[g][...]
        for j in range(3):
            put_slabs(sc, j, rows, qkv_ref[j, g].astype(F32))
        put_slabs(sc, 3, rows, dot(d_attn, wp_ref[...], NT).astype(BF16).astype(F32))

        def image(s, carry):
            return attn_bwd_image(sc, dsc, masks, s, carry)

        lax.fori_loop(0, GI, image, 0, unroll=True)
        total = (prev0, prev1)[g][...].astype(F32) if not first else None
        for j in range(3):
            d_j = jnp.concatenate(
                [dsc[2 * j, 0:rows, :], dsc[2 * j + 1, 0:rows, :]], axis=1
            ).astype(BF16)
            dqkv_ref[j, g] = d_j
            part = dot(d_j, wq_ref[j], NT)
            total = part if total is None else total + part
        (own_ref, other_ref)[g][...] = total.astype(BF16)


def attn_bwd(d_own, d_other, prev, qkv, w_qkv, w_proj):
    d = w_qkv.shape[1]
    hc = w_qkv.shape[2]
    rows = NVIS * GI
    one = jax.ShapeDtypeStruct((rows, d), BF16)
    first = prev is None
    outs = [jax.ShapeDtypeStruct((3, 2, rows, hc), BF16), one, one]
    ins = [d_own, d_other] + ([] if first else list(prev)) + [qkv, w_qkv, w_proj]
    return pl.pallas_call(
        functools.partial(attn_bwd_kernel, first, rows),
        out_shape=outs,
        grid=(1,),
        in_specs=[whole(a.shape) for a in ins],
        out_specs=[whole(o.shape) for o in outs],
        scratch_shapes=[
            pltpu.VMEM((8, QPAD * GI, 128), F32),
            pltpu.VMEM((6, QPAD * GI, 128), F32),
        ],
        compiler_params=params(48),
        cost_estimate=cost(2 * 2 * rows * d * hc * 7, 10 * MIB),
        name="attn_bwd",
    )(*ins)


def join(pieces):
    return jnp.concatenate([p[...] for p in pieces], axis=1)


def mlp_kernel(a0, a1, p0, p1, p2, p3, w1, b1, w2, e0, e1, e2, e3, *outs):
    mlp0, mlp1, dh0, dh1, hid, dup, dmlp, gb = outs
    i = pl.program_id(0)
    a = jnp.where(i == 0, a0[...], a1[...])
    demb = jnp.concatenate([p0[0], p1[0], p2[0], p3[0]], axis=1)
    dm = dot(demb, join((e0, e1, e2, e3)), NT).astype(BF16)
    dmlp[0] = dm
    width = w1.shape[1]
    for f in range(0, width, 256):
        cols = slice(f, f + 256)
        up = dot(a, w1[:, cols]) + b1[:, cols]
        cdf = 0.5 * (1.0 + lax.erf(up * SQRT_HALF))
        hid[0, :, cols] = (up * cdf).astype(BF16)
        d_hid = dot(dm, w2[cols, :], NT)
        pdf = jnp.exp(up * up * -0.5) * INV_SQRT_2PI
        d_up = (d_hid * (cdf + up * pdf)).astype(BF16)
        dup[0, :, cols] = d_up
        s = jnp.sum(d_up.astype(F32), axis=0, keepdims=True)
        gb[:, cols] = jnp.where(i == 0, s, gb[:, cols] + s)
    dh = dot(dup[0], w1[...], NT).astype(BF16)
    mlp = dot(hid[0], w2[...]).astype(BF16)
    for r, (m_ref, d_ref) in enumerate(((mlp0, dh0), (mlp1, dh1))):

        @pl.when(i == r)
        def _():
            m_ref[...] = mlp
            d_ref[...] = dh


def mlp_pair(base, a_first, a_second, pieces, w1, b1, w2, we):
    rows, d = a_first.shape
    f = w1.shape[1]
    ec = pieces[0].shape[2]
    one = jax.ShapeDtypeStruct((rows, d), BF16)
    pair = jax.ShapeDtypeStruct((2, rows, d), BF16)
    hidden = jax.ShapeDtypeStruct((2, rows, f), BF16)
    step = lambda n: pl.BlockSpec((1, rows, n), lambda i: (i, 0, 0))
    piece = lambda r: pl.BlockSpec((1, rows, ec), lambda i: ((base + i) ^ r, 0, 0))
    return pl.pallas_call(
        mlp_kernel,
        out_shape=[one] * 4 + [hidden, hidden, pair, jax.ShapeDtypeStruct((1, f), F32)],
        grid=(2,),
        in_specs=[whole((rows, d))] * 2
        + [piece(r) for r in range(4)]
        + [whole(w1.shape), whole(b1.shape), whole(w2.shape)]
        + [whole(w.shape) for w in we],
        out_specs=[whole((rows, d))] * 4 + [step(f), step(f), step(d), whole((1, f))],
        compiler_params=params(48),
        cost_estimate=cost(2 * 2 * rows * d * f * 4.5, 18 * MIB, 4 * rows * f),
        name="mlp_pair",
    )(a_first, a_second, *pieces, w1, b1, w2, *we)


def own_rows(x_ref, c, k0, k1):
    lo, hi = image_rows(x_ref, k0, k1)
    return jnp.where(c == 0, lo, hi)


def ln2_kernel(meta, x_ref, keep, recv, g_ref, b_ref, x1_ref, a_ref, x_own):
    for k0 in range(0, NVIS, 7):
        sl = slice(k0 * GI, (k0 + 7) * GI)
        x = own_rows(x_ref, meta[1], k0, k0 + 7)
        x_own[sl, :] = x.astype(BF16)
        x1 = x + (
            keep[sl, :].astype(F32) + recv[sl, :].astype(F32)
        )
        x1_ref[sl, :] = x1
        a_ref[sl, :] = (normalize(x1)[0] * g_ref[...] + b_ref[...]).astype(BF16)


def ln2(meta, x3, part, recv, gain, shift):
    rows, d = recv.shape
    return pl.pallas_call(
        ln2_kernel,
        out_shape=[jax.ShapeDtypeStruct((rows, d), F32)] + [jax.ShapeDtypeStruct((rows, d), BF16)] * 2,
        grid_spec=pltpu.PrefetchScalarGridSpec(
            num_scalar_prefetch=1,
            grid=(1,),
            in_specs=[
                pl.BlockSpec((NVIS, 2 * GI, d), lambda i, m: (0, m[0], 0)),
                whole((rows, d)),
                whole((rows, d)),
                whole((1, d)),
                whole((1, d)),
            ],
            out_specs=[whole((rows, d))] * 3,
        ),
        compiler_params=params(32),
        cost_estimate=cost(20 * rows * d, 6 * MIB),
        name="ln2",
    )(meta, x3, part, recv, gain, shift)


def backward_rows(x, d_out, gain):
    xhat, inv = normalize(x)
    e = d_out * gain
    d_x = inv * (
        e
        - jnp.mean(e, axis=-1, keepdims=True)
        - xhat * jnp.mean(e * xhat, axis=-1, keepdims=True)
    )
    return d_x, jnp.sum(d_out * xhat, axis=0, keepdims=True), jnp.sum(d_out, axis=0, keepdims=True)


def ln2_bwd_kernel(
    x1, keep, r1, r2, p0, p1, p2, p3, e0, e1, e2, e3, g_ref, dx1, dattn, gg, gb
):
    rows = x1.shape[0]
    we = join((e0, e1, e2, e3))
    gg[...] = jnp.zeros_like(gg)
    gb[...] = jnp.zeros_like(gb)
    for r0 in range(0, rows, 56):
        sl = slice(r0, r0 + 56)
        demb = jnp.concatenate([p[0, sl, :] for p in (p0, p1, p2, p3)], axis=1)
        d_h = keep[sl, :].astype(F32) + r1[sl, :].astype(F32) + r2[sl, :].astype(F32)
        d_x, s_g, s_b = backward_rows(x1[sl, :], d_h, g_ref[...])
        d_x = d_x + dot(demb, we, NT)
        dx1[sl, :] = d_x
        dattn[sl, :] = d_x.astype(BF16)
        gg[...] += s_g
        gb[...] += s_b


def ln2_bwd(x1, dh2, r1, r2, pieces, we, gain):
    rows, d = x1.shape
    ec = pieces[0].shape[2]
    piece = lambda r: pl.BlockSpec((1, rows, ec), lambda i: (r, 0, 0))
    vec = jax.ShapeDtypeStruct((1, d), F32)
    return pl.pallas_call(
        ln2_bwd_kernel,
        out_shape=[
            jax.ShapeDtypeStruct((rows, d), F32),
            jax.ShapeDtypeStruct((rows, d), BF16),
            vec,
            vec,
        ],
        grid=(1,),
        in_specs=[
            whole((rows, d)),
            whole((rows, d)),
            whole((rows, d)),
            whole((rows, d)),
        ]
        + [piece(r) for r in range(4)]
        + [whole(w.shape) for w in we]
        + [whole((1, d))],
        out_specs=[whole((rows, d)), whole((rows, d)), whole((1, d)), whole((1, d))],
        compiler_params=params(32),
        cost_estimate=cost(2 * rows * d * DEC, 8 * MIB),
        name="ln2_bwd",
    )(x1, dh2, r1, r2, *pieces, *we, gain)


def ln1_bwd_kernel(meta, x_ref, dx1, keep, recv, g_ref, out, gg, gb):
    gg[...] = jnp.zeros_like(gg)
    gb[...] = jnp.zeros_like(gb)
    for k0 in range(0, NVIS, 7):
        sl = slice(k0 * GI, (k0 + 7) * GI)
        d_h = keep[sl, :].astype(F32) + recv[sl, :].astype(F32)
        d_x, s_g, s_b = backward_rows(own_rows(x_ref, meta[1], k0, k0 + 7), d_h, g_ref[...])
        out[sl, :] = (dx1[sl, :] + d_x).astype(BF16)
        gg[...] += s_g
        gb[...] += s_b


def ln1_bwd(meta, x3, dx1, dh1, recv, gain):
    rows, d = dx1.shape
    vec = jax.ShapeDtypeStruct((1, d), F32)
    return pl.pallas_call(
        ln1_bwd_kernel,
        out_shape=[jax.ShapeDtypeStruct((rows, d), BF16), vec, vec],
        grid_spec=pltpu.PrefetchScalarGridSpec(
            num_scalar_prefetch=1,
            grid=(1,),
            in_specs=[
                pl.BlockSpec((NVIS, 2 * GI, d), lambda i, m: (0, m[0], 0)),
                whole((rows, d)),
                whole((rows, d)),
                whole((rows, d)),
                whole((1, d)),
            ],
            out_specs=[whole((rows, d)), whole((1, d)), whole((1, d))],
        ),
        compiler_params=params(32),
        cost_estimate=cost(20 * rows * d, 6 * MIB),
        name="ln1_bwd",
    )(meta, x3, dx1, dh1, recv, gain)


def assemble_kernel(meta, g0, g1, g2, g3, out):
    i = pl.program_id(0)
    for r, g in enumerate((g0, g1, g2, g3)):

        @pl.when(i == r)
        def _():
            out[...] = g[...].astype(F32).reshape(out.shape)


def assemble(meta, groups):
    rows, d = groups[0].shape
    return pl.pallas_call(
        assemble_kernel,
        out_shape=jax.ShapeDtypeStruct((NVIS, 4 * GI, d), F32),
        grid_spec=pltpu.PrefetchScalarGridSpec(
            num_scalar_prefetch=1,
            grid=(4,),
            in_specs=[whole((rows, d))] * 4,
            out_specs=pl.BlockSpec((NVIS, GI, d), lambda i, m: (0, i ^ m[2], 0)),
        ),
        compiler_params=params(32),
        cost_estimate=cost(rows * d, 10 * MIB),
        name="assemble",
    )(meta, *groups)


def out_embed_kernel(x1, keep, r1, r2, e0, e1, e2, e3, z_ref, emb):
    mlp = keep[...].astype(F32) + r1[...].astype(F32) + r2[...].astype(F32)
    z = (x1[...] + mlp).astype(BF16)
    z_ref[...] = z
    e = dot(z, join((e0, e1, e2, e3))).astype(BF16)
    ec = emb.shape[2]
    for q in range(4):
        emb[q] = e[:, q * ec : (q + 1) * ec]


def out_embed(x1, mlp, r1, r2, we):
    rows, d = x1.shape
    ec = we[0].shape[1]
    return pl.pallas_call(
        out_embed_kernel,
        out_shape=[
            jax.ShapeDtypeStruct((rows, d), BF16),
            jax.ShapeDtypeStruct((4, rows, ec), BF16),
        ],
        grid=(1,),
        in_specs=[
            whole((rows, d)),
            whole((rows, d)),
            whole((rows, d)),
            whole((rows, d)),
        ]
        + [whole(w.shape) for w in we],
        out_specs=[whole((rows, d)), whole((4, rows, ec))],
        compiler_params=params(32),
        cost_estimate=cost(2 * rows * d * DEC, 6 * MIB),
        name="out_embed",
    )(x1, mlp, r1, r2, *we)


def collect_kernel(recv_index, cot, po, rows_out, token, csc):
    csc[...] = cot[...].astype(F32).reshape(csc.shape)
    total = jnp.sum(csc[...], axis=0, keepdims=True)
    if rows_out.shape[0] > cot.shape[1]:
        rows_out[...] = jnp.zeros_like(rows_out)
    images = cot.shape[1]
    lane = lax.broadcasted_iota(jnp.int32, (KPAD, GRID), 1)

    def image(g, seen):
        cells = csc[pl.ds(g, GRID, stride=images), :].astype(BF16)
        pick = jnp.where(po[g] == lane, 1.0, 0.0).astype(BF16)
        v = dot(pick, cells)
        rows_out[recv_index[g]] = v.astype(BF16)
        return seen + jnp.sum(v, axis=0, keepdims=True)

    seen = lax.fori_loop(0, images, image, jnp.zeros((1, 128), F32), unroll=4)
    token[...] = total - seen


def collect(recv_index, cot, po_cols, slots):
    return pl.pallas_call(
        collect_kernel,
        out_shape=[
            jax.ShapeDtypeStruct((slots, KPAD, 128), BF16),
            jax.ShapeDtypeStruct((1, 128), F32),
        ],
        grid_spec=pltpu.PrefetchScalarGridSpec(
            num_scalar_prefetch=1,
            grid=(1,),
            in_specs=[whole(cot.shape), whole(po_cols.shape)],
            out_specs=[whole((slots, KPAD, 128)), whole((1, 128))],
            scratch_shapes=[pltpu.VMEM((GRID * cot.shape[1], 128), F32)],
        ),
        compiler_params=params(32),
        cost_estimate=cost(2 * 32 * KPAD * GRID * 128, 4 * MIB),
        name="collect",
    )(recv_index, cot, po_cols)


def to_rows_kernel(meta, index, slots, out, sc):
    rows = out.shape[1]
    for s in range(4 * GI):
        v = slots[index[s]].astype(F32)
        sc[(s // GI) ^ meta[2], pl.ds(s % GI, KPAD, stride=GI), :] = v
    out[...] = sc[:, 0:rows, :].astype(BF16)


def to_rows(meta, index, slots):
    rows = NVIS * GI
    return pl.pallas_call(
        to_rows_kernel,
        out_shape=jax.ShapeDtypeStruct((4, rows, 128), BF16),
        grid_spec=pltpu.PrefetchScalarGridSpec(
            num_scalar_prefetch=2,
            grid=(1,),
            in_specs=[whole(slots.shape)],
            out_specs=whole((4, rows, 128)),
            scratch_shapes=[pltpu.VMEM((4, KPAD * GI, 128), F32)],
        ),
        compiler_params=params(16),
        cost_estimate=cost(4 * rows * 128, MIB),
        name="to_rows",
    )(meta, index, slots)


def to_slots_kernel(meta, index, e0, e1, e2, e3, out, sc):
    rows = e0.shape[-2]
    for r, e in enumerate((e0, e1, e2, e3)):
        sc[r, 0:rows, :] = e[...].reshape(rows, 128).astype(F32)
    sc[:, rows:, :] = jnp.zeros((4, KPAD * GI - rows, 128), F32)
    if out.shape[0] > 4 * GI:
        out[...] = jnp.zeros_like(out)
    for s in range(4 * GI):
        v = sc[(s // GI) ^ meta[2], pl.ds(s % GI, KPAD, stride=GI), :]
        out[index[s]] = v.astype(BF16)


def to_slots(meta, index, emb, received, slots):
    rows = NVIS * GI
    return pl.pallas_call(
        to_slots_kernel,
        out_shape=jax.ShapeDtypeStruct((slots, KPAD, 128), BF16),
        grid_spec=pltpu.PrefetchScalarGridSpec(
            num_scalar_prefetch=2,
            grid=(1,),
            in_specs=[pl.BlockSpec((1, rows, 128), lambda *_: (0, 0, 0))] + [whole((rows, 128))] * 3,
            out_specs=whole((slots, KPAD, 128)),
            scratch_shapes=[pltpu.VMEM((4, KPAD * GI, 128), F32)],
        ),
        compiler_params=params(16),
        cost_estimate=cost(4 * rows * 128, MIB),
        name="to_slots",
    )(meta, index, emb, *received)


def grid_kernel(meta, index, slots, po, token, table, out, sc):
    images = out.shape[1]
    cell = lax.broadcasted_iota(jnp.int32, (GRID, KPAD), 0)
    ones = jnp.ones((KPAD, 128), BF16)

    def image(g, carry):
        pick = jnp.where(po[g] == cell, 1.0, 0.0).astype(BF16)
        both = dot(pick, jnp.concatenate([slots[index[g]], ones], axis=1))
        v = jnp.where(both[:, 128:] > 0.5, both[:, :128], token[...])
        sc[pl.ds(g, GRID, stride=images), :] = v
        return carry

    lax.fori_loop(0, images, image, 0, unroll=4)

    def line(i, carry):
        for j in range(SIDE):
            u = jnp.where(meta[2] < 2, i, j)
            p = i * SIDE + j
            start = pl.multiple_of(p * images, images)
            out[p] = sc[pl.ds(start, images), :] + table[u]
        return carry

    lax.fori_loop(0, SIDE, line, 0)


def grid_out(meta, index, slots, po_rows, token, table):
    images = table.shape[1]
    return pl.pallas_call(
        grid_kernel,
        out_shape=jax.ShapeDtypeStruct((GRID, images, 128), F32),
        grid_spec=pltpu.PrefetchScalarGridSpec(
            num_scalar_prefetch=2,
            grid=(1,),
            in_specs=[whole(slots.shape), whole(po_rows.shape), whole((1, 128)), whole(table.shape)],
            out_specs=whole((GRID, images, 128)),
            scratch_shapes=[pltpu.VMEM((GRID * images, 128), F32)],
        ),
        compiler_params=params(32),
        cost_estimate=cost(2 * 32 * KPAD * GRID * 256, 5 * MIB),
        name="grid_out",
    )(meta, index, slots, po_rows, token, table)


def position_table(level_index, part):
    sample = GSD_LOW * jnp.exp(
        level_index.astype(F32) * (math.log(GSD_HIGH / GSD_LOW) / (GSD_LEVELS - 1))
    )
    quarter = DEC // 4
    angular = jnp.exp(jnp.arange(quarter).astype(F32) * (-math.log(10000.0) / quarter))
    coordinate = jnp.arange(SIDE).astype(F32)
    phase = sample[None, :, None] * (coordinate[:, None] * angular[None, :])[:, None, :]
    return jnp.where(part % 2 == 1, jnp.cos(phase), jnp.sin(phase))


def after(v, *others):
    return lax.optimization_barrier((v,) + others)[0]


def put_halves(swap, lo, hi, send, keep, at=()):
    send[(0, *at)] = jnp.where(swap, lo, hi).astype(BF16)
    keep[(0, *at)] = jnp.where(swap, hi, lo).astype(BF16)


def grad_kernel(split_rows, n, place, *refs):
    a_refs, b_refs, (send, keep) = refs[:n], refs[n : 2 * n], refs[2 * n :]
    total = None
    for a, b in zip(a_refs, b_refs):
        for g in range(a.shape[0]):
            t = dot(a[g], b[g], TN)
            total = t if total is None else total + t
    swap = place[0] == 1
    if split_rows:
        half = total.shape[0] // 2
        put_halves(swap, total[:half], total[half:], send, keep)
    else:
        half = total.shape[1] // 2
        put_halves(swap, total[:, :half], total[:, half:], send, keep)


def grad_weight(place, a_list, b_list, split_rows):
    rows = a_list[0].shape[1]
    m, n = a_list[0].shape[2], b_list[0].shape[2]
    if split_rows:
        a_spec = lambda g: pl.BlockSpec((g, rows, m // 4), lambda i, p: (0, 0, i))
        b_spec = lambda g: pl.BlockSpec((g, rows, n), lambda i, p: (0, 0, 0))
        shape = (4, m // 8, n)
    else:
        a_spec = lambda g: pl.BlockSpec((g, rows, m), lambda i, p: (0, 0, 0))
        b_spec = lambda g: pl.BlockSpec((g, rows, n // 4), lambda i, p: (0, 0, i))
        shape = (4, m, n // 8)
    return pl.pallas_call(
        functools.partial(grad_kernel, split_rows, len(a_list)),
        out_shape=[jax.ShapeDtypeStruct(shape, BF16)] * 2,
        grid_spec=pltpu.PrefetchScalarGridSpec(
            num_scalar_prefetch=1,
            grid=(4,),
            in_specs=[a_spec(a.shape[0]) for a in a_list] + [b_spec(b.shape[0]) for b in b_list],
            out_specs=[pl.BlockSpec((1,) + shape[1:], lambda i, p: (i ^ p[1], 0, 0))] * 2,
        ),
        compiler_params=params(48),
        cost_estimate=cost(2 * rows * m * n * sum(a.shape[0] for a in a_list), 8 * MIB),
        name="grad_weight",
    )(place, *a_list, *b_list)


def grad_qkv_kernel(place, a_ref, b_ref, send, keep):
    cols = b_ref.shape[3]
    swap = place[0] == 1
    for j in range(3):
        total = dot(a_ref[0], b_ref[j, 0], TN) + dot(a_ref[1], b_ref[j, 1], TN)
        half = total.shape[0] // 2
        put_halves(
            swap,
            total[:half],
            total[half:],
            send,
            keep,
            (slice(None), slice(j * cols, (j + 1) * cols)),
        )


def grad_qkv_weight(place, a, b):
    _, rows, m = a.shape
    cols = b.shape[3]
    shape = (4, m // 8, 3 * cols)
    return pl.pallas_call(
        grad_qkv_kernel,
        out_shape=[jax.ShapeDtypeStruct(shape, BF16)] * 2,
        grid_spec=pltpu.PrefetchScalarGridSpec(
            num_scalar_prefetch=1,
            grid=(4,),
            in_specs=[pl.BlockSpec((2, rows, m // 4), lambda i, p: (0, 0, i)), whole(b.shape)],
            out_specs=[pl.BlockSpec((1,) + shape[1:], lambda i, p: (i ^ p[1], 0, 0))] * 2,
        ),
        compiler_params=params(32),
        cost_estimate=cost(2 * 2 * rows * m * 3 * cols, 6 * MIB),
        name="grad_qkv",
    )(place, a, b)


MESH = pl.DeviceIdType.MESH
CHUNKS = [(0, 80), (80, 160), (160, 240), (240, 320), (320, 392)]


def flip(v, s):
    if s == 0:
        return v
    if s == 1:
        return v + 1 - 2 * lax.rem(v, 2)
    if s == 2:
        return lax.rem(v + 2, 4)
    return 3 - v


def add32(*refs):
    total = refs[0].astype(F32)
    for v in refs[1:]:
        total = total + v.astype(F32)
    return total


def main_kernel(names, *refs):
    r = types.SimpleNamespace(**dict(zip(names, refs)))
    d, t = lax.axis_index("dp"), lax.axis_index("tensor")
    x, z = lax.rem(d, 2), lax.div(d, 2)
    core, far = {"tensor": flip(t, 1)}, {"tensor": flip(t, 2)}
    beside = {"dp": d + 1 - 2 * x}
    along = [None] + [{"dp": 2 * flip(z, s) + x} for s in (1, 2, 3)]
    n_local, n_remote = itertools.count(), itertools.count()
    sent = []

    def fetch(src, dst):
        copy = pltpu.make_async_copy(src, dst, r.lsem.at[next(n_local)])
        copy.start()
        return copy

    def remote(src, dst, peer):
        n = next(n_remote)
        copy = pltpu.make_async_remote_copy(
            src_ref=src,
            dst_ref=dst,
            send_sem=r.ssem.at[n],
            recv_sem=r.rsem.at[n],
            device_id=peer,
            device_id_type=MESH,
        )
        sent.append(copy)
        return copy

    def send(src, dst, peer):
        copy = remote(src, dst, peer)
        copy.start()
        return copy

    def left(copy):
        copy.wait_send()
        sent[:] = [c for c in sent if c is not copy]

    ld_p = [fetch(getattr(r, f"p{k}"), r.P.at[k]) for k in range(4)]
    ld_we = [fetch(getattr(r, f"e{k}"), r.WE.at[:, 128 * k : 128 * (k + 1)]) for k in range(4)]
    ld_a2 = fetch(r.a2, r.A2.at[0])
    ld_w1 = fetch(r.w1, r.W1)
    ld_w2 = fetch(r.w2, r.W2)
    ld_x1 = fetch(r.x1, r.X1)
    ld_wp = [fetch(r.wpn, r.WP.at[0]), fetch(r.wpf, r.WP.at[1])]

    peers = [core, far, beside] + along[1:]
    barrier = pltpu.get_barrier_semaphore()
    for p in peers:
        pl.semaphore_signal(barrier, inc=1, device_id=p, device_id_type=MESH)
    pl.semaphore_wait(barrier, len(peers))

    a2_far = send(r.a2, r.A2.at[2], far)
    a2_core = send(r.a2, r.A2.at[1], core)
    a2_both = remote(r.A2.at[2], r.A2.at[3], core)
    dh_near = remote(r.DH.at[1], r.DHC.at[0], core)
    mlp_near = remote(r.MLP.at[1], r.MLPC.at[0], core)

    for c in ld_p + ld_we:
        c.wait()

    def d_mlp(g, carry):
        demb = jnp.concatenate([r.P[k, flip(g, k)] for k in range(4)], axis=1)
        r.DM[g] = dot(demb, r.WE[...], NT).astype(BF16)
        return carry

    lax.fori_loop(0, 4, d_mlp, 0)
    for c in (ld_a2, ld_w1, ld_w2):
        c.wait()

    def mlp(g, gb):
        @pl.when(g == 1)
        def _():
            a2_core.wait_recv()

        @pl.when(g == 2)
        def _():
            a2_far.wait_recv()
            a2_both.start()

        @pl.when(g == 3)
        def _():
            a2_both.wait_recv()

        a, dm = r.A2[g], r.DM[g]
        sums = []
        for f in range(0, r.W1.shape[1], 256):
            cols = slice(f, f + 256)
            up = dot(a, r.W1[:, cols]) + r.b1[:, cols]
            cdf = 0.5 * (1.0 + lax.erf(up * SQRT_HALF))
            r.HID[g, :, cols] = (up * cdf).astype(BF16)
            d_hid = dot(dm, r.W2[cols, :], NT)
            pdf = jnp.exp(up * up * -0.5) * INV_SQRT_2PI
            d_up = (d_hid * (cdf + up * pdf)).astype(BF16)
            r.DUP[g, :, cols] = d_up
            sums.append(jnp.sum(d_up.astype(F32), axis=0, keepdims=True))
        r.DH[g] = dot(r.DUP[g], r.W1[...], NT).astype(BF16)
        r.MLP[g] = dot(r.HID[g], r.W2[...]).astype(BF16)

        @pl.when(g == 1)
        def _():
            dh_near.start()
            mlp_near.start()

        return gb + jnp.concatenate(sums, axis=1)

    r.SM[4:5, :] = lax.fori_loop(0, 4, mlp, jnp.zeros((1, r.W1.shape[1]), F32))

    dh_far = send(r.DH.at[3], r.DHC.at[1], core)
    mlp_far = send(r.MLP.at[3], r.MLPC.at[1], core)
    dh_far.wait_recv()
    r.DH[2] = add32(r.DH[2], r.DHC[1]).astype(BF16)
    dh_y = send(r.DH.at[2], r.DHY, far)
    mlp_far.wait_recv()
    r.MLP[2] = add32(r.MLP[2], r.MLPC[1]).astype(BF16)
    mlp_y = send(r.MLP.at[2], r.MLPY, far)

    ld_wq = []
    for w_ref, w in ((r.W2, r.wqn), (r.W1, r.wqf)):
        ld_wq.append([fetch(w.at[j], w_ref.at[:, 256 * j : 256 * (j + 1)]) for j in range(3)])

    def halves(total, axis):
        lo, hi = (total[:128], total[128:]) if axis == 0 else (total[:, :128], total[:, 128:])
        return jnp.where(x == 1, lo, hi).astype(BF16), jnp.where(x == 1, hi, lo).astype(BF16)

    def z_cols(k):
        return pl.ds(pl.multiple_of(256 * flip(z, k), 256), 256)

    ORDER = (1, 2, 3, 0)
    x_fc1, x_fc2, z_fc1, z_fc2 = {}, {}, [], []
    for k in ORDER:
        total = None
        for g in range(4):
            v = dot(r.A2[g, :, z_cols(k)], r.DUP[g], TN)
            total = v if total is None else total + v
        r.S1[k], r.K1[k] = halves(total, 0)
        x_fc1[k] = send(r.S1.at[k], r.X1B.at[k], beside)
    left(a2_both)
    left(a2_core)
    left(a2_far)
    ld_a1 = [fetch(r.a1.at[g], r.A2.at[g]) for g in range(2)]
    ld_att = [
        fetch(att.at[g], r.A2.at[2 + s, :, 256 * g : 256 * (g + 1)])
        for s, att in enumerate((r.attn, r.attf))
        for g in range(2)
    ]

    def fc1_on(k):
        x_fc1[k].wait_recv()
        r.K1[k] = add32(r.K1[k], r.X1B[k]).astype(BF16)
        z_fc1.append(send(r.K1.at[k], r.Z1.at[k - 1], along[k]))

    def fc2_on(k):
        x_fc2[k].wait_recv()
        r.K2[k] = add32(r.K2[k], r.X2B[k]).astype(BF16)
        z_fc2.append(send(r.K2.at[k], r.Z2.at[k - 1], along[k]))

    for k in ORDER:
        total = None
        for g in range(4):
            v = dot(r.HID[g], r.DM[g, :, z_cols(k)], TN)
            total = v if total is None else total + v
        r.S2[k], r.K2[k] = halves(total, 1)
        x_fc2[k] = send(r.S2.at[k], r.X2B.at[k], beside)
        if k == 0:
            fc1_on(1)

    ld_qkv = [
        fetch(q.at[j, g], r.DM.at[2 * s + g, :, 256 * j : 256 * (j + 1)])
        for s, q in enumerate((r.qkvn, r.qkvf))
        for g in range(2)
        for j in range(3)
    ]

    dh_near.wait_recv()
    dh_y.wait_recv()
    ld_x1.wait()
    gg = gs = jnp.zeros((1, r.X1.shape[1]), F32)
    for a, b in CHUNKS:
        d_h = add32(r.DH[0, a:b], r.DHC[0, a:b], r.DHY[a:b])
        d_x, s_g, s_b = backward_rows(r.X1[a:b], d_h, r.g2[...])
        demb = jnp.concatenate([r.P[k, k, a:b] for k in range(4)], axis=1)
        d_x = d_x + dot(demb, r.WE[...], NT)
        r.DAT[0, a:b] = d_x.astype(BF16)
        gg, gs = gg + s_g, gs + s_b
    r.SM[2:3, :] = gg
    r.SM[3:4, :] = gs
    d_attn = send(r.DAT.at[0], r.DAT.at[1], core)
    fc1_on(2)
    fc1_on(3)
    for c in ld_wp + ld_att + ld_a1 + ld_wq[0] + ld_wq[1] + ld_qkv:
        c.wait()
    d_attn.wait_recv()

    x_proj, z_proj = [None, None], [[], []]
    for s in (1, 0):
        for k in ORDER:
            total = None
            for g in range(2):
                v = dot(r.A2[2 + s, :, 256 * g : 256 * (g + 1)], r.DAT[g, :, z_cols(k)], TN)
                total = v if total is None else total + v
            r.DUP[k, 0:256, 128 * s : 128 * (s + 1)], r.KP[s, k] = halves(total, 1)
        x_proj[s] = send(r.DUP.at[:, 0:256, 128 * s : 128 * (s + 1)], r.XP.at[s], beside)

    def proj_on(s):
        x_proj[s].wait_recv()
        for k in (1, 2, 3):
            r.KP[s, k] = add32(r.KP[s, k], r.XP[s, k]).astype(BF16)
            z_proj[s].append(send(r.KP.at[s, k], r.ZP.at[s, k - 1], along[k]))

    left(dh_near)
    masks = head_masks()
    rows = r.DAT.shape[1]
    r.SC[:, rows:, :] = jnp.zeros((8, r.SC.shape[1] - rows, 128), F32)

    def attention(s):
        wq = (r.W2, r.W1)[s]
        for g in (1, 0):
            for j in range(3):
                put_slabs(r.SC, j, rows, r.DM[2 * s + g, :, 256 * j : 256 * (j + 1)].astype(F32))
            put_slabs(r.SC, 3, rows, dot(r.DAT[g], r.WP[s], NT).astype(BF16).astype(F32))
            lax.fori_loop(
                0, GI, lambda i, c: attn_bwd_image(r.SC, r.DSC, masks, i, c), 0, unroll=4
            )
            total = r.DH[g].astype(F32) if s == 0 else None
            for j in range(3):
                d_j = jnp.concatenate(
                    [r.DSC[2 * j, 0:rows, :], r.DSC[2 * j + 1, 0:rows, :]], axis=1
                ).astype(BF16)
                r.HID[2 * s + g, :, 256 * j : 256 * (j + 1)] = d_j
                part = dot(d_j, wq[:, 256 * j : 256 * (j + 1)], NT)
                total = part if total is None else total + part
            r.DH[g] = total.astype(BF16)

    def qkv_block(s, k):
        total = None
        for g in range(2):
            v = dot(r.A2[g, :, z_cols(k)], r.HID[2 * s + g, :, 0:768], TN)
            total = v if total is None else total + v
        return total

    attention(1)
    y_qkv, x_qkv, z_qkv = {}, {}, []
    for k in ORDER:
        r.DUP[k, 0:256, 256:1024] = qkv_block(1, k).astype(BF16)
        y_qkv[k] = send(r.DUP.at[k, 0:256, 256:1024], r.RQ.at[k], far)
    fc2_on(1)
    for c in x_fc1.values():
        left(c)

    left(mlp_near)
    mlp_near.wait_recv()
    mlp_y.wait_recv()
    r.MLP[1] = (r.X1[...] + add32(r.MLP[0], r.MLPC[0], r.MLPY[...])).astype(BF16)
    emb = dot(r.MLP[1], r.WE[...]).astype(BF16)
    for q in range(4):
        r.EMB[q] = emb[:, 128 * q : 128 * (q + 1)]
    e_core = send(r.EMB.at[1], r.EM.at[0], core)
    e_y2 = send(r.EMB.at[3], r.EF, far)
    e_y = send(r.EMB.at[2], r.EM.at[1], far)
    ld_xo = fetch(r.xo, r.MLP.at[0])
    fc2_on(2)
    fc2_on(3)

    attention(0)
    dh1 = send(r.DH.at[1], r.DHC.at[1], core)
    e_y2.wait_recv()
    e_both = send(r.EF, r.EM.at[2], core)

    def qkv_near(k):
        total = qkv_block(0, k)
        y_qkv[k].wait_recv()
        out = r.S1.at[k, :, 0:768]
        out[...], r.KQ[k] = halves(total + r.RQ[k].astype(F32), 0)
        x_qkv[k] = send(out, r.XQ.at[k], beside)

    def qkv_on(k):
        x_qkv[k].wait_recv()
        r.KQ[k] = add32(r.KQ[k], r.XQ[k]).astype(BF16)
        z_qkv.append(send(r.KQ.at[k], r.ZQ.at[k - 1], along[k]))

    qkv_near(1)

    left(mlp_y)
    ld_xo.wait()
    dh1.wait_recv()
    gg = gs = jnp.zeros((1, r.X1.shape[1]), F32)
    for a, b in CHUNKS:
        d_h = add32(r.DH[0, a:b], r.DHC[1, a:b])
        d_x, s_g, s_b = backward_rows(r.MLP[0, a:b].astype(F32), d_h, r.g1[...])
        r.MLP[2, a:b] = (r.DAT[0, a:b].astype(F32) + d_x).astype(BF16)
        gg, gs = gg + s_g, gs + s_b
    r.SM[0:1, :] = gg
    r.SM[1:2, :] = gs
    g_y = send(r.MLP.at[2], r.gi2, far)
    g_core = send(r.MLP.at[2], r.gi1, core)
    ld_gi = fetch(r.MLP.at[2], r.gi0)
    r.SM[5:6, :] = jnp.concatenate(
        [r.token[...], jnp.zeros((1, r.SM.shape[1] - 128), F32)], axis=1
    )
    r.SM[6:8, :] = jnp.zeros((2, r.SM.shape[1]), F32)
    sm_x = send(r.SM, r.SMR.at[0], beside)
    proj_on(1)
    proj_on(0)
    qkv_near(2)

    e_core.wait_recv()
    e_y.wait_recv()
    e_both.wait_recv()
    r.SC[0, 0:rows, :] = r.EMB[0].astype(F32)
    for k in range(3):
        r.SC[k + 1, 0:rows, :] = r.EM[k].astype(F32)
    for slot in range(r.SL.shape[0]):
        v = r.SC[r.slot_group[slot], pl.ds(r.slot_row[slot], KPAD, stride=GI), :]
        r.SL[slot] = v.astype(BF16)
    per = r.SL.shape[0] // 8
    mine = pl.ds(d * per, per)
    moved = []
    for k in range(4):
        for h in range(2):
            other = 2 * flip(z, k) + (x if h == 0 else 1 - x)
            there = pl.ds(other * per, per)
            if k == 0 and h == 0:
                ld_own = fetch(r.SL.at[there], r.slots.at[mine])
            else:
                moved.append(send(r.SL.at[there], r.slots.at[mine], {"dp": other}))

    demb = jnp.concatenate([r.P[k, k] for k in range(4)], axis=1)
    for k in ORDER:
        total = dot(r.MLP[1, :, z_cols(k)], demb, TN)
        parts = halves(total, 0)
        for h, v in enumerate(parts):
            r.GE[h, k] = jnp.concatenate([v[:, :128], v[:, 256:384]], axis=1)
            r.GC[h, k] = jnp.concatenate([v[:, 128:256], v[:, 384:]], axis=1)
    ge_core = send(r.GC, r.GR, core)
    qkv_on(1)
    sm_x.wait_recv()
    r.SM2[...] = r.SM[...] + r.SMR[0]
    sm_z = [send(r.SM2, r.SMR.at[k], along[k]) for k in (1, 2, 3)]
    ge_core.wait_recv()
    r.GE[...] = add32(r.GE[...], r.GR[...]).astype(BF16)
    ge_x = send(r.GE.at[0], r.XE, beside)
    qkv_near(3)
    qkv_on(2)
    for c in sm_z:
        c.wait_recv()
    r.SM3[...] = r.SM2[...] + r.SMR[1] + r.SMR[2] + r.SMR[3]
    sm_core = send(r.SM3, r.SMR.at[4], core)
    ge_x.wait_recv()
    z_ge = []
    for k in (1, 2, 3):
        r.GE[1, k] = add32(r.GE[1, k], r.XE[k]).astype(BF16)
        z_ge.append(send(r.GE.at[1, k], r.ZE.at[k - 1], along[k]))
    sm_core.wait_recv()
    r.SM4[...] = r.SM3[...] + r.SMR[4]
    sm_y = send(r.SM4, r.SMR.at[5], far)
    qkv_near(0)
    qkv_on(3)

    for c in z_proj[1] + z_proj[0] + z_ge:
        c.wait_recv()
    r.FP[...] = add32(r.KP[1, 0], r.XP[1, 0], r.ZP[1, 0], r.ZP[1, 1], r.ZP[1, 2]).astype(BF16)
    y_proj = send(r.FP, r.YP, far)
    two = add32(r.GE[1, 0], r.XE[0], r.ZE[0], r.ZE[1], r.ZE[2])
    r.FE[...] = two[:, 128:].astype(BF16)
    y_emb = send(r.FE, r.YE, far)
    g_y.wait_recv()
    g_both = send(r.gi2, r.gi3, core)
    for c in [x_fc1[0], x_fc2[0]] + z_fc1 + z_fc2:
        c.wait_recv()
    r.o_fc1[...] = add32(r.K1[0], r.X1B[0], r.Z1[0], r.Z1[1], r.Z1[2])
    r.o_fc2[...] = add32(r.K2[0], r.X2B[0], r.Z2[0], r.Z2[1], r.Z2[2])
    y_proj.wait_recv()
    r.o_proj[...] = add32(
        r.KP[0, 0], r.XP[0, 0], r.ZP[0, 0], r.ZP[0, 1], r.ZP[0, 2], r.YP[...]
    )
    y_emb.wait_recv()
    r.o_emb[...] = two[:, :128] + r.YE[...].astype(F32)
    sm_y.wait_recv()
    r.o_sum[0:4] = r.SM4[0:4] + r.SMR[5, 0:4]
    r.o_sum[4:8] = r.SM3[4:8]
    x_qkv[0].wait_recv()
    for c in z_qkv:
        c.wait_recv()
    own = add32(r.KQ[0], r.XQ[0], r.ZQ[0], r.ZQ[1], r.ZQ[2])
    for j in range(3):
        r.o_qkv[j] = own[:, 256 * j : 256 * (j + 1)]
    g_core.wait_recv()
    g_both.wait_recv()
    for c in moved:
        c.wait_recv()
    for c in (ld_own, ld_gi):
        c.wait()
    for c in sent:
        c.wait_send()


def main_call(ins, g1, g2, b1, token, slot_group, slot_row):
    rows, width = ins["a2"].shape
    bf = lambda *s: jax.ShapeDtypeStruct(s, BF16)
    f32 = lambda *s: jax.ShapeDtypeStruct(s, F32)
    vm = lambda *s: pltpu.VMEM(s, BF16)
    vf = lambda *s: pltpu.VMEM(s, F32)
    small = dict(g1=g1, g2=g2, b1=b1, token=token)
    scalars = dict(slot_group=slot_group, slot_row=slot_row)
    outs = {f"gi{k}": bf(rows, width) for k in range(4)}
    count = slot_group.shape[0]
    outs["slots"] = bf(count, KPAD, 128)
    dense = dict(
        o_fc1=f32(128, width),
        o_fc2=f32(width, 128),
        o_proj=f32(256, 128),
        o_qkv=f32(3, 128, 256),
        o_emb=f32(128, 128),
        o_sum=f32(8, width),
    )
    scratch = dict(
        P=vm(4, 4, rows, 128),
        WE=vm(width, 512),
        W1=vm(width, width),
        W2=vm(width, width),
        WP=vm(2, 256, width),
        A2=vm(4, rows, width),
        HID=vm(4, rows, width),
        DUP=vm(4, rows, width),
        DM=vm(4, rows, width),
        DH=vm(4, rows, width),
        MLP=vm(4, rows, width),
        DHC=vm(2, rows, width),
        MLPC=vm(2, rows, width),
        DHY=vm(rows, width),
        MLPY=vm(rows, width),
        X1=vf(rows, width),
        DAT=vm(2, rows, width),
        SC=vf(8, QPAD * GI, 128),
        DSC=vf(6, QPAD * GI, 128),
        S1=vm(4, 128, width),
        K1=vm(4, 128, width),
        X1B=vm(4, 128, width),
        Z1=vm(3, 128, width),
        S2=vm(4, width, 128),
        K2=vm(4, width, 128),
        X2B=vm(4, width, 128),
        Z2=vm(3, width, 128),
        KP=vm(2, 4, 256, 128),
        XP=vm(2, 4, 256, 128),
        ZP=vm(2, 3, 256, 128),
        FP=vm(256, 128),
        YP=vm(256, 128),
        RQ=vm(4, 256, 768),
        KQ=vm(4, 128, 768),
        XQ=vm(4, 128, 768),
        ZQ=vm(3, 128, 768),
        EM=vm(3, rows, 128),
        SL=vm(count, KPAD, 128),
        EMB=vm(4, rows, 128),
        EF=vm(rows, 128),
        GE=vm(2, 4, 128, 256),
        GC=vm(2, 4, 128, 256),
        GR=vm(2, 4, 128, 256),
        XE=vm(4, 128, 256),
        ZE=vm(3, 128, 256),
        FE=vm(128, 128),
        YE=vm(128, 128),
        SM=vf(8, width),
        SM2=vf(8, width),
        SM3=vf(8, width),
        SM4=vf(8, width),
        SMR=vf(6, 8, width),
        lsem=pltpu.SemaphoreType.DMA((64,)),
        ssem=pltpu.SemaphoreType.DMA((96,)),
        rsem=pltpu.SemaphoreType.DMA((96,)),
    )
    names = list(ins) + list(small) + list(scalars) + list(outs) + list(dense) + list(scratch)
    anywhere = pl.BlockSpec(memory_space=pl.ANY)
    in_vmem = pl.BlockSpec(memory_space=pltpu.VMEM)
    res = pl.pallas_call(
        functools.partial(main_kernel, names),
        out_shape=list(outs.values()) + list(dense.values()),
        in_specs=[anywhere] * len(ins)
        + [in_vmem] * len(small)
        + [pl.BlockSpec(memory_space=pltpu.SMEM)] * len(scalars),
        out_specs=[anywhere] * len(outs) + [in_vmem] * len(dense),
        scratch_shapes=list(scratch.values()),
        compiler_params=pltpu.CompilerParams(
            vmem_limit_bytes=63 * MIB, collective_id=0, has_side_effects=True
        ),
        cost_estimate=cost(2e10, 50 * MIB),
        name="layer_main",
    )(*ins.values(), *small.values(), *scalars.values())
    return types.SimpleNamespace(**dict(zip(list(outs) + list(dense), res)))


def local(
    encoder_input,
    ln1_gain,
    ln1_bias,
    qkv_weight,
    proj_weight,
    ln2_gain,
    ln2_bias,
    fc1_weight,
    fc1_bias,
    fc2_weight,
    embed_weight,
    mask_token,
    grid_cotangent,
    image_order,
    patch_order,
    gsd_index,
):
    ndp = lax.axis_size("dp")
    d = lax.axis_index("dp")
    t = lax.axis_index("tensor")
    images, _, width = encoder_input.shape
    rows = NVIS * GI
    xbit, zpos = d % 2, d // 2
    meta = jnp.stack([t // 2, t % 2, t]).astype(jnp.int32)

    def over_core(v):
        return lax.ppermute(v, "tensor", [(i, i ^ 1) for i in range(4)])

    def over_y(v):
        return lax.ppermute(v, "tensor", [(i, i ^ 2) for i in range(4)])

    def over_x(v):
        return lax.ppermute(v, "dp", [(i, i ^ 1) for i in range(ndp)])

    pick = functools.partial(lax.dynamic_index_in_dim, axis=0, keepdims=False)

    g1 = ln1_gain.astype(F32)[None, :]
    s1 = ln1_bias.astype(F32)[None, :]
    g2 = ln2_gain.astype(F32)[None, :]
    s2 = ln2_bias.astype(F32)[None, :]
    bias_up = fc1_bias.astype(F32)[None, :]
    x3 = encoder_input.transpose(1, 0, 2)
    cot = grid_cotangent.transpose(1, 0, 2)
    w_qkv = qkv_weight.transpose(1, 0, 2)

    def y_half(w, axis):
        half = w.shape[axis] // 2
        return over_y(lax.dynamic_slice_in_dim(w, xbit * half, half, axis))

    def both_halves(mine, axis):
        other = over_x(mine)
        lo = jnp.where(xbit == 0, mine, other)
        hi = jnp.where(xbit == 0, other, mine)
        return jnp.concatenate([lo, hi], axis=axis)

    half_qk = y_half(w_qkv[:2], 1)
    half_v = y_half(w_qkv[2:], 1)
    half_proj = y_half(proj_weight, 0)
    we_core = over_core(embed_weight)
    we_y = over_y(embed_weight)

    capacity = max(1, images // ndp)
    slots = ndp * capacity
    own_images = lax.dynamic_slice_in_dim(image_order, d * images, images)
    dest = own_images // images
    before = jnp.arange(images)[None, :] < jnp.arange(images)[:, None]
    rank = jnp.sum((dest[:, None] == dest[None, :]) & before, axis=1)
    send_index = (dest * capacity + rank).astype(jnp.int32)
    every = jnp.arange(image_order.shape[0])
    wanted = d * images + jnp.arange(images)
    slot = jnp.sum(jnp.where(image_order[None, :] == wanted[:, None], every[None, :], 0), axis=1)
    source = slot // images
    to_me = image_order // images == d
    earlier = (
        to_me[None, :]
        & (every[None, :] // images == source[:, None])
        & (every[None, :] < slot[:, None])
    )
    recv_index = (source * capacity + jnp.sum(earlier, axis=1)).astype(jnp.int32)

    visible = jnp.pad(
        patch_order[:, :NVIS], ((0, 0), (0, KPAD - NVIS)), constant_values=-1
    )

    def over_dp(v):
        return lax.all_to_all(v, "dp", split_axis=0, concat_axis=0, tiled=True)

    back, token_grad = collect(recv_index, cot, visible[:, :, None], slots)
    back = over_dp(back)
    p0 = to_rows(meta, send_index, back)
    p1, p2 = over_core(p0), over_y(p0)

    w_qk_far = both_halves(half_qk, 1)
    g1_later = after(g1, half_qk, p0)
    a1, qkv_a, att_a, own_a, other_a = attn_fwd(
        meta, True, [x3, g1_later, s1], w_qkv, proj_weight
    )
    half_v, half_proj = after(half_v, a1), after(half_proj, a1)
    w_qkv_far = jnp.concatenate([w_qk_far, both_halves(half_v, 1)], axis=0)
    w_proj_far = both_halves(half_proj, 0)
    we_y, p2 = after(we_y, a1), after(p2, a1)
    we = (embed_weight, we_core, we_y, over_core(we_y))
    p3 = over_core(p2)
    pieces = (p0, p1, p2, p3)
    table = position_table(gsd_index, t)
    qkv_b, att_b, own_b, other_b = attn_fwd(
        meta, False, [after(a1, table), own_a, other_a], w_qkv_far, w_proj_far
    )
    x1, a2, x_own = ln2(meta, x3, own_b, over_core(other_b), g2, s2)
    if ndp == 8:
        source_slot = jnp.sum(
            jnp.where(
                send_index[None, :] == jnp.arange(slots)[:, None], jnp.arange(images)[None, :], 0
            ),
            axis=1,
        )
        main = main_call(
            dict(
                zip(["p0", "p1", "p2", "p3"], pieces),
                **dict(zip(["e0", "e1", "e2", "e3"], we)),
                a2=a2,
                x1=x1,
                xo=x_own,
                w1=fc1_weight,
                w2=fc2_weight,
                wpn=proj_weight,
                wpf=w_proj_far,
                wqn=w_qkv,
                wqf=w_qkv_far,
                a1=a1,
                attn=att_a,
                attf=att_b,
                qkvn=qkv_a,
                qkvf=qkv_b,
            ),
            g1,
            g2,
            bias_up,
            token_grad,
            ((source_slot // GI) ^ t).astype(jnp.int32),
            (source_slot % GI).astype(jnp.int32),
        )
        grid_features = grid_out(
            meta,
            recv_index,
            main.slots,
            visible[:, None, :],
            mask_token.astype(F32)[None, :],
            table,
        )
        grad_input = assemble(meta, (main.gi0, main.gi1, main.gi2, main.gi3))
        return (
            grid_features.transpose(1, 0, 2),
            grad_input.transpose(1, 0, 2),
            main.o_sum[0],
            main.o_sum[1],
            main.o_qkv.transpose(1, 0, 2),
            main.o_proj,
            main.o_sum[2],
            main.o_sum[3],
            main.o_fc1,
            main.o_sum[4],
            main.o_fc2,
            main.o_emb,
            main.o_sum[5, :128],
        )

    a2_y = over_y(a2)
    a2_core = over_core(a2)

    mlp0, mlp1, dh0, dh1, hid_n, dup_n, dm_n, gb_n = mlp_pair(
        0, a2, a2_core, pieces, fc1_weight, bias_up, fc2_weight, we
    )
    dh_core, mlp_core = over_core(dh1), over_core(mlp1)
    a2_y = after(a2_y, dh0)
    a2_far = over_core(a2_y)
    mlp2, mlp3, dh2, dh3, hid_f, dup_f, dm_f, gb_f = mlp_pair(
        2, a2_y, a2_far, pieces, fc1_weight, bias_up, fc2_weight, we
    )

    def add16(a, b):
        return (a.astype(F32) + b.astype(F32)).astype(BF16)

    fast = ndp == 8
    place = jnp.stack([xbit, zpos]).astype(jnp.int32) if fast else jnp.zeros((2,), jnp.int32)

    def stage_x(parts):
        send, keep = parts
        return keep, over_x(send) if fast else send

    def stage_z(held, *done):
        if not fast:
            return held
        keep, got = held
        got = after(got, *done)
        arrived = [
            lax.ppermute(add16(keep[s], got[s]), "dp", [(i, i ^ (2 * s)) for i in range(8)])
            for s in range(1, 4)
        ]
        return keep[0].astype(F32) + got[0].astype(F32), arrived

    def stage_sum(held, axis, *done):
        if not fast:
            flat = jnp.stack(held, axis=1)
            if axis == 1:
                flat = flat.transpose(2, 0, 1, 3)
                flat = flat.reshape(flat.shape[0], -1)
            else:
                flat = flat.reshape(-1, flat.shape[-1])
            return lax.psum_scatter(flat, "dp", scatter_dimension=axis, tiled=True).astype(F32)
        total, arrived = held
        for v in after(tuple(arrived), *done):
            total = total + v.astype(F32)
        return total

    def pairs(v):
        return [v[0:1], v[1:2]]

    dh_sum = add16(dh2, over_core(dh3))
    dh_y = over_y(dh_sum)
    fc2_w = grad_weight(place, [after(hid_n, dh_sum), hid_f], [dm_n, dm_f], False)
    fc2_x = stage_x(fc2_w)
    mlp_sum = add16(after(mlp2, fc2_w[0]), over_core(mlp3))
    mlp_y = over_y(mlp_sum)
    a2_parts = [after(a2, mlp_sum)[None], a2_core[None], a2_y[None], a2_far[None]]
    fc1_w = grad_weight(place, a2_parts, pairs(dup_n) + pairs(dup_f), True)
    fc1_x = stage_x(fc1_w)

    dx1, d_attn, gg2, gs2 = ln2_bwd(x1, after(dh0, fc1_w[0]), dh_core, dh_y, pieces, we, g2)
    d_attn_core = over_core(d_attn)
    d_pair = [d_attn[None], d_attn_core[None]]
    proj_far_w = grad_weight(place, pairs(att_b), d_pair, False)
    proj_far_x = stage_x(proj_far_w)
    proj_near_w = grad_weight(place, pairs(after(att_a, proj_far_w[0])), d_pair, False)
    proj_near_x = stage_x(proj_near_w)
    dqkv_b, own_b, other_b = attn_bwd(
        after(d_attn, proj_near_w[0]), d_attn_core, None, qkv_b, w_qkv_far, w_proj_far
    )
    qkv_far_w = grad_qkv_weight(place, a1, dqkv_b)
    qkv_far_x = stage_x(qkv_far_w)
    fc2_z = stage_z(fc2_x, qkv_far_w[0])
    z, emb = out_embed(after(x1, fc2_z[0]), mlp0, mlp_core, mlp_y, we)
    e_core, e2 = over_core(emb[1]), over_y(emb[2:4])
    dqkv_a, own_a, other_a = attn_bwd(
        after(d_attn, z), d_attn_core, (own_b, other_b), qkv_a, w_qkv, proj_weight
    )
    dh1_core = over_core(other_a)
    qkv_near_w = grad_qkv_weight(place, a1, dqkv_a)
    qkv_near_x = stage_x(qkv_near_w)
    fc1_z = stage_z(fc1_x, qkv_near_w[0])
    g_own, gg1, gs1 = ln1_bwd(meta, x3, after(dx1, fc1_z[0]), own_a, dh1_core, g1)
    g_y = over_y(g_own)
    g_core = over_core(g_own)
    small = jnp.concatenate(
        [gg1, gs1, gg2, gs2, gb_n + gb_f, jnp.pad(token_grad, ((0, 0), (0, width - 128)))], axis=0
    )
    step = 1
    while step < ndp:
        small = small + lax.ppermute(small, "dp", [(i, i ^ step) for i in range(ndp)])
        step *= 2
    sums = small[:4] + over_core(small[:4])
    sums = sums + over_y(sums)
    gb, token_sum = small[4:5], small[5:6, :128]

    e2 = after(e2, g_own)
    sent = to_slots(meta, send_index, emb, (e_core, e2[0], over_core(e2[1])), slots)
    arrived = over_dp(sent)
    qkv_far_z = stage_z(qkv_far_x, arrived)
    proj_far_z = stage_z(proj_far_x, arrived)
    proj_near_z = stage_z(proj_near_x, arrived)
    demb_own = jnp.concatenate([p[r : r + 1] for r, p in enumerate(pieces)], axis=2)
    ec = embed_weight.shape[1]
    embed_w = grad_weight(place, [after(z, arrived)[None]], [demb_own], True)
    embed_w = [
        add16(
            jnp.concatenate([v[..., :ec], v[..., 2 * ec : 3 * ec]], axis=-1),
            over_core(jnp.concatenate([v[..., ec : 2 * ec], v[..., 3 * ec :]], axis=-1)),
        )
        for v in embed_w
    ]
    embed_x = stage_x(embed_w)
    grid_features = grid_out(
        meta,
        recv_index,
        after(arrived, embed_w[0]),
        visible[:, None, :],
        mask_token.astype(F32)[None, :],
        table,
    )
    qkv_near_z = stage_z(qkv_near_x, grid_features)
    embed_z = stage_z(embed_x, grid_features)

    def over_pair(near, far):
        return near + over_y(far.astype(BF16)).astype(F32)

    grad_fc2 = stage_sum(fc2_z, 1, grid_features)
    grad_fc1 = stage_sum(fc1_z, 0, grid_features)
    grad_proj = over_pair(
        stage_sum(proj_near_z, 1, grid_features), stage_sum(proj_far_z, 1, grid_features)
    )
    grad_qkv = over_pair(
        stage_sum(qkv_near_z, 0, grid_features), stage_sum(qkv_far_z, 0, grid_features)
    )
    hc = qkv_weight.shape[2]
    grad_qkv = jnp.stack([grad_qkv[:, j * hc : (j + 1) * hc] for j in range(3)], axis=1)
    embed_two = stage_sum(embed_z, 0)
    grad_embed = over_pair(embed_two[:, :ec], embed_two[:, ec:])
    grad_input = assemble(meta, (g_own, g_core, g_y, over_core(g_y)))
    return (
        grid_features.transpose(1, 0, 2),
        grad_input.transpose(1, 0, 2),
        sums[0],
        sums[1],
        grad_qkv,
        grad_proj,
        sums[2],
        sums[3],
        grad_fc1,
        gb[0],
        grad_fc2,
        grad_embed,
        token_sum[0],
    )


def solution(mesh):
    return jax.shard_map(
        local,
        mesh=mesh,
        in_specs=(
            P("dp", None, None),
            P(),
            P(),
            P(None, None, "tensor"),
            P("tensor", None),
            P(),
            P(),
            P(None, "tensor"),
            P("tensor"),
            P("tensor", None),
            P(None, "tensor"),
            P("tensor"),
            P("dp", None, "tensor"),
            P(),
            P("dp", None),
            P("dp"),
        ),
        out_specs=(
            P("dp", None, "tensor"),
            P("dp", None, None),
            P(),
            P(),
            P("dp", None, "tensor"),
            P("tensor", "dp"),
            P(),
            P(),
            P("dp", "tensor"),
            P("tensor"),
            P("tensor", "dp"),
            P("dp", "tensor"),
            P("tensor"),
        ),
        check_vma=False,
    )
```
